256 devices in a mesh: seq: 16 (over x, y), head: 16 (over z, core).
Axes of the slice: x: 4, y: 4, z: 8, core: 2. Of those that a mesh axis runs over, the one named last changes fastest.
Arguments:
- activations: bfloat16 [65536, 768], P(('seq', 'head')), may hold values from -6 to 6
- ln_gain: bfloat16 [768], replicated, may hold values from 0.099609375 to 1.8984375
- w_query: bfloat16 [768, 768], replicated
- w_key: bfloat16 [768, 768], replicated
- w_value: bfloat16 [768, 768], replicated, may hold values from -0.21875 to 0.21875
- w_gate: bfloat16 [768, 768], replicated, may hold values from -0.21875 to 0.21875
- w_out: bfloat16 [768, 768], replicated, may hold values from -0.21875 to 0.21875
- bias_tiles: bfloat16 [16, 16, 128, 256], P(None, 'head'), may hold values from -6 to 6
- crop_lengths: int32 [16], replicated, may hold values from 1 to 16384, 65536 in all
- tile_index: int32 [512], P('seq'), may hold values from 0 to 15
- d_out: bfloat16 [65536, 768], P(('seq', 'head')), may hold values from -6 to 6
Outputs:
- d_activations: bfloat16 [65536, 768], P(('seq', 'head'))
- d_bias: float32 [16, 16, 128, 256], P(None, 'head')
The draws below stay inside these ranges and needn't reach their ends.
Inputs may be any that keep to these rules, and one draw needn't show every extreme that they name: crop_lengths sum to 65536; the longest crop is exactly 16384 rows.
All inputs are finite; a program needn't handle non-finite values.
Results may differ from the reference program's by a relative error of at most 0.039.
The reference program's roundings to bfloat16 on the way count: a program that leaves them out, or rounds other values in their place, can miss the bound.
Values may be sent and summed in bfloat16 or wider, within the bound.
A program may use at most 128 MiB of HBM per device.

```python
import math
import jax
import jax.numpy as jnp
import numpy as np
from jax import lax

D = 768
HEADS = 16
DH = 48
BLOCK = 128
NTILES = 16
CROPS = 16
TOKENS = 65536
BLOCKS = 512


def shared_parts(key):
    base = jnp.clip(jax.random.normal(jax.random.fold_in(key, 71), (D, D), jnp.float32), -6.0, 6.0)
    other = jnp.clip(jax.random.normal(jax.random.fold_in(key, 72), (D, D), jnp.float32), -6.0, 6.0)
    return (base, other)


def draw_w_query(key, part):
    base, other = shared_parts(key)
    result = base * D ** (-0.5)
    return result.astype(jnp.bfloat16)


def draw_w_key(key, part):
    base, other = shared_parts(key)
    result = other * D ** (-0.5)
    return result.astype(jnp.bfloat16)


def plant(values, key, least, top_value):
    dims = values.shape
    spot = [jax.random.randint(jax.random.fold_in(key, axis), (), 0, dims[axis]) for axis in range(len(dims))]
    values = values.at[tuple(spot)].set(least)
    longest = dims.index(max(dims))
    spot[longest] = (spot[longest] + 1) % dims[longest]
    return values.at[tuple(spot)].set(top_value)


def block_scale(rng, dims, cuts, low, high):
    def one(axis_at, blocks):
        heights = jax.random.uniform(jax.random.fold_in(jax.random.fold_in(rng, 6), axis_at), (blocks,), jnp.float32, low / len(cuts), high / len(cuts))
        return jnp.repeat(jnp.exp(heights), dims[axis_at] // blocks).reshape((-1,) + (1,) * (len(dims) - axis_at - 1))

    gain = one(*cuts[0])
    for cut in cuts[1:]:
        gain = gain * one(*cut)
    return gain


def split_up(count, total, reach, skew):
    loads = [(1 << 20) // math.isqrt(rank ** skew) + 1 for rank in range(2, count + 1)]
    spare, holding = total - reach - (count - 1), [1] * (count - 1)
    while spare > 0:
        movable = [i for i in range(count - 1) if holding[i] < reach]
        mass, left = sum([loads[i] for i in movable]), spare
        for i in movable:
            extra = min(reach - holding[i], max(1, left * loads[i] // mass), spare)
            holding[i] = holding[i] + extra
            spare = spare - extra
    return np.array([reach] + holding)


def uneven(rng, amount, total, limit, slope):
    if amount == 2:
        one = jax.random.randint(rng, (), max(1, total - limit), min(limit, total - 1) + 1)
        return jnp.stack([one, total - one])
    sizes = jnp.asarray(split_up(amount, total, limit, slope), jnp.int32)
    couples = (amount - 1) // 2
    giver, taker = sizes[1:1 + 2 * couples:2], sizes[2:2 + 2 * couples:2]
    room = jnp.minimum(giver - 1, limit - taker)
    passed = jax.random.randint(jax.random.fold_in(rng, 1), (couples,), 0, 1 << 20) % (room + 1)
    sizes = sizes.at[1:1 + 2 * couples:2].set(giver - passed).at[2:2 + 2 * couples:2].set(taker + passed)
    return sizes[jax.random.permutation(jax.random.fold_in(rng, 2), amount)]


def noise(own_key, shape, deviation, reach, cuts=(), kind=jnp.bfloat16):
    values = deviation * jax.random.normal(own_key, shape, jnp.float32)
    if cuts:
        values = values * block_scale(own_key, shape, cuts, -0.22, 0.18)
    return jnp.clip(values, -reach, reach).astype(kind)


def setup_inputs(seed: int = 0) -> dict:
    key_list = jax.random.split(jax.random.key(seed), 12)
    activations = noise(key_list[0], (TOKENS, D), 1.0, 6.0, ((0, 256),))
    ln_gain = jnp.clip(1.0 + 0.18 * jax.random.normal(key_list[1], (D,), jnp.float32), 0.099609375, 1.8984375).astype(jnp.bfloat16)
    w_query = draw_w_query(jax.random.fold_in(key_list[11], 71), 0)
    w_key = draw_w_key(jax.random.fold_in(key_list[11], 71), 0)
    w_value = noise(key_list[4], (D, D), D ** -0.5, 0.21875)
    w_gate = noise(key_list[5], (D, D), D ** -0.5, 0.21875)
    w_out = noise(key_list[6], (D, D), D ** -0.5, 0.21875)
    bias_tiles = noise(key_list[7], (NTILES, HEADS, BLOCK, 2 * BLOCK), 1.0, 6.0, ((1, 16),))
    crop_lengths = uneven(key_list[8], CROPS, TOKENS, TOKENS // 4, 2).astype(jnp.int32)
    tile_index = plant(jax.random.randint(key_list[9], (BLOCKS,), 0, NTILES), jax.random.fold_in(key_list[9], 1), 0, NTILES - 1).astype(jnp.int32)
    d_out = noise(key_list[10], (TOKENS, D), 1.0, 6.0, ((0, 256),))
    return dict(activations=activations, ln_gain=ln_gain, w_query=w_query, w_key=w_key, w_value=w_value, w_gate=w_gate, w_out=w_out, bias_tiles=bias_tiles, crop_lengths=crop_lengths, tile_index=tile_index, d_out=d_out)


eps = 1e-05

def norm_rows(activations, ln_gain):
    values = activations.astype(jnp.float32)
    centred = values - lax.optimization_barrier(jnp.mean(values, axis=1, keepdims=True))
    inverse = lax.rsqrt(lax.optimization_barrier(jnp.mean(centred * centred, axis=1, keepdims=True)) + eps)
    scaled = centred * inverse
    normed = (scaled * ln_gain.astype(jnp.float32)[None, :]).astype(jnp.bfloat16)
    return (normed, scaled, inverse)

def norm_back(d_normed, scaled, inverse, ln_gain):
    d_scaled = d_normed * ln_gain.astype(jnp.float32)[None, :]
    centre = lax.optimization_barrier(jnp.mean(d_scaled, axis=1, keepdims=True))
    along = lax.optimization_barrier(jnp.mean(d_scaled * scaled, axis=1, keepdims=True))
    return (inverse * (d_scaled - centre - scaled * along)).astype(jnp.bfloat16)

def window_mask(first, blocks, crop_lengths):
    bounds = jnp.cumsum(crop_lengths).astype(jnp.int32)

    def crop_of(positions):
        return lax.optimization_barrier(jnp.sum((bounds[None, :] <= positions[:, None]).astype(jnp.int32), axis=1))
    queries = first + jnp.arange(blocks * BLOCK, dtype=jnp.int32)
    starts = first + BLOCK * jnp.arange(blocks, dtype=jnp.int32) - BLOCK
    key_pos = starts[:, None] + jnp.arange(2 * BLOCK, dtype=jnp.int32)[None, :]
    query_crop = crop_of(queries).reshape(blocks, BLOCK)
    key_crop = crop_of(key_pos.reshape(-1)).reshape(blocks, 2 * BLOCK)
    return (key_pos >= 0)[:, None, :] & (query_crop[:, :, None] == key_crop[:, None, :])

def as_wide(array):
    return array.astype(jnp.float32)

def attention_pass(queries, keys, values, keys_before, values_before, grad_out, bias, allowed, heads_here):
    rows, width = queries.shape
    blocks = rows // BLOCK
    size = width // heads_here
    scale = 1.0 / math.sqrt(size)

    def split(array):
        return array.reshape(blocks, BLOCK, heads_here, size)
    query_blocks = split(queries)
    key_blocks = split(keys)
    value_blocks = split(values)
    grad_blocks = split(grad_out)
    key_prev = jnp.concatenate([keys_before.reshape(1, BLOCK, heads_here, size), key_blocks[:-1]], axis=0)
    value_prev = jnp.concatenate([values_before.reshape(1, BLOCK, heads_here, size), value_blocks[:-1]], axis=0)
    key_window = jnp.concatenate([key_prev, key_blocks], axis=1)
    value_window = jnp.concatenate([value_prev, value_blocks], axis=1)
    mask = allowed[:, None, :, :]
    scores = jnp.einsum('nihd,njhd->nhij', as_wide(query_blocks), as_wide(key_window)) * scale + bias
    scores = jnp.where(mask, scores, -1e+30)
    top = lax.optimization_barrier(jnp.max(scores, axis=3, keepdims=True))
    weights = jnp.where(mask, jnp.exp(scores - top), 0.0)
    probs = weights / lax.optimization_barrier(jnp.sum(weights, axis=3, keepdims=True))
    probs_low = probs.astype(jnp.bfloat16)
    attended = jnp.einsum('nhij,njhd->nihd', as_wide(probs_low), as_wide(value_window))
    attended = attended.astype(jnp.bfloat16).reshape(rows, width)
    d_probs = jnp.einsum('nihd,njhd->nhij', as_wide(grad_blocks), as_wide(value_window))
    d_scores = probs * (d_probs - lax.optimization_barrier(jnp.sum(probs * d_probs, axis=3, keepdims=True)))
    d_low = d_scores.astype(jnp.bfloat16)
    d_queries = jnp.einsum('nhij,njhd->nihd', as_wide(d_low), as_wide(key_window)) * scale
    d_queries = d_queries.astype(jnp.bfloat16).reshape(rows, width)
    d_key_window = jnp.einsum('nhij,nihd->njhd', as_wide(d_low), as_wide(query_blocks)) * scale
    d_value_window = jnp.einsum('nhij,nihd->njhd', as_wide(probs_low), as_wide(grad_blocks))
    empty = jnp.zeros((1, BLOCK, heads_here, size), jnp.float32)
    d_keys = d_key_window[:, BLOCK:] + jnp.concatenate([d_key_window[1:, :BLOCK], empty], axis=0)
    d_values = d_value_window[:, BLOCK:] + jnp.concatenate([d_value_window[1:, :BLOCK], empty], axis=0)
    return (attended, d_queries, d_keys.reshape(rows, width), d_values.reshape(rows, width), d_key_window[0, :BLOCK].reshape(BLOCK, width), d_value_window[0, :BLOCK].reshape(BLOCK, width), d_scores)

def reference(activations, ln_gain, w_query, w_key, w_value, w_gate, w_out, bias_tiles, crop_lengths, tile_index, d_out):
    normed, scaled, inverse = norm_rows(activations, ln_gain)
    queries = jnp.dot(normed, w_query, preferred_element_type=jnp.float32).astype(jnp.bfloat16)
    keys = jnp.dot(normed, w_key, preferred_element_type=jnp.float32).astype(jnp.bfloat16)
    values = jnp.dot(normed, w_value, preferred_element_type=jnp.float32).astype(jnp.bfloat16)
    gate_input = jnp.dot(normed, w_gate, preferred_element_type=jnp.float32).astype(jnp.bfloat16)
    d_mixed = jnp.dot(d_out, w_out.T, preferred_element_type=jnp.float32).astype(jnp.bfloat16)
    gate = jax.nn.sigmoid(gate_input.astype(jnp.float32))
    grad_out = (d_mixed.astype(jnp.float32) * gate).astype(jnp.bfloat16)
    allowed = window_mask(jnp.int32(0), TOKENS // BLOCK, crop_lengths)
    picks = (tile_index[:, None] == jnp.arange(NTILES, dtype=jnp.int32)[None, :]).astype(jnp.float32)
    empty_block = jnp.zeros((BLOCK, DH), jnp.bfloat16)

    def heads_first(array):
        return array.reshape(TOKENS, HEADS, DH).transpose(1, 0, 2)

    def per_head(pieces):
        head_q, head_k, head_v, head_g, head_tiles = pieces
        bias = jnp.einsum('nt,tij->nij', picks, head_tiles.astype(jnp.float32))[:, None]
        results = attention_pass(head_q, head_k, head_v, empty_block, empty_block, head_g, bias, allowed, 1)
        d_tiles = jnp.einsum('nt,nij->tij', picks, results[6][:, 0], precision=lax.Precision.HIGHEST)
        return (results[0], results[1], results[2], results[3], d_tiles)
    attended, d_queries, d_keys, d_values, d_tiles = lax.map(per_head, (heads_first(queries), heads_first(keys), heads_first(values), heads_first(grad_out), bias_tiles.transpose(1, 0, 2, 3)))

    def rows_first(array):
        return array.transpose(1, 0, 2).reshape(TOKENS, D)
    attended = rows_first(attended)
    d_queries = rows_first(d_queries)
    d_keys = rows_first(d_keys).astype(jnp.bfloat16)
    d_values = rows_first(d_values).astype(jnp.bfloat16)
    d_gate = (d_mixed.astype(jnp.float32) * attended.astype(jnp.float32) * gate * (1.0 - gate)).astype(jnp.bfloat16)
    d_normed = jnp.dot(d_queries, w_query.T, preferred_element_type=jnp.float32)
    d_normed = d_normed + jnp.dot(d_keys, w_key.T, preferred_element_type=jnp.float32)
    d_normed = d_normed + jnp.dot(d_values, w_value.T, preferred_element_type=jnp.float32)
    d_normed = d_normed + jnp.dot(d_gate, w_gate.T, preferred_element_type=jnp.float32)
    d_activations = norm_back(d_normed, scaled, inverse, ln_gain)
    return (d_activations, d_tiles.transpose(1, 0, 2, 3))
```

```python
import functools
import math

import jax
import jax.numpy as jnp
from jax import lax
from jax.experimental import pallas as pl
from jax.experimental.pallas import tpu as pltpu
from jax.sharding import PartitionSpec as P

MESH = pl.DeviceIdType.MESH
F32 = jnp.float32
BF16 = jnp.bfloat16
EPS = 1e-05
UNSEEN = -1e30
BLOCK = 128
PAIR = 2 * BLOCK


def mm(a, b, dims):
    return lax.dot_general(a, b, (dims, ((), ())), preferred_element_type=F32)


def kernel(
    H, S, DH,
    act_ref, gain_ref, dout_ref, wq_hbm, wk_hbm, wv_hbm, wg_hbm, wo_hbm, bias_ref,
    lengths_ref, tiles_ref, chain_ref, last_ref,
    dact_ref, dbias_ref,
    wq, wk, wv, wg, wo, normed, scaled, inverse, gin, dmix, send, recv, res, got,
    own, nxt, chain, hotq, hotk, edge_out, edge_in, parts, parts_in, summed, dnorm,
    w_sem, f_send, f_recv, b_send, b_recv, r_send, r_recv, a_send, a_recv, e_send, e_recv,
):
    s, h = lax.axis_index("seq"), lax.axis_index("head")
    D = H * DH
    half_heads = H // 2
    half_cols = half_heads * DH
    scale = 1.0 / math.sqrt(DH)
    q_rows, k_rows, v_rows, g_rows = (pl.ds(i * DH, DH) for i in range(4))
    kv_rows = pl.ds(DH, 2 * DH)
    last_block = pl.ds(BLOCK, BLOCK)

    def wrap(i, n):
        return lax.rem(i + n, n)

    barrier = pltpu.get_barrier_semaphore()
    for o in range(1, H):
        pl.semaphore_signal(barrier, inc=1, device_id=(s, wrap(h + o, H)), device_id_type=MESH)
    for o in range(1, S):
        pl.semaphore_signal(barrier, inc=1, device_id=(wrap(s + o, S), h), device_id_type=MESH)

    loads = [
        pltpu.make_async_copy(a, b, w_sem.at[i])
        for i, (a, b) in enumerate(
            ((wq_hbm, wq), (wk_hbm, wk), (wv_hbm, wv), (wg_hbm, wg), (wo_hbm, wo))
        )
    ]
    for load in loads:
        load.start()

    gain = gain_ref[...].astype(F32)
    x = act_ref[...].astype(F32)
    centred = x - jnp.mean(x, axis=1, keepdims=True)
    inv = lax.rsqrt(jnp.mean(centred * centred, axis=1, keepdims=True) + EPS)
    xhat = centred * inv
    scaled[...] = xhat
    inverse[...] = jnp.broadcast_to(inv, inverse.shape)
    normed[...] = (xhat * gain).astype(BF16)

    def forward_copy(t):
        return pltpu.make_async_remote_copy(
            send.at[t], recv.at[h + 1], f_send.at[t], f_recv.at[h],
            device_id=(s, t), device_id_type=MESH,
        )

    def forward_arrival(j):
        return pltpu.make_async_remote_copy(
            send.at[j], recv.at[j + 1], f_send.at[j], f_recv.at[j],
            device_id=(s, j), device_id_type=MESH,
        )

    own_copy = pltpu.make_async_copy(send.at[h], recv.at[h + 1], f_recv.at[h])
    offsets = []
    for i in range(H - 1):
        offsets.append(-(i // 2 + 1) if i % 2 == 0 else i // 2 + 1)

    def by_head(product):
        return product.T.astype(BF16).reshape(half_heads, DH, PAIR)

    my_half = h // half_heads
    for turn in range(2):
        half = my_half if turn == 0 else 1 - my_half
        cols = pl.ds(pl.multiple_of(half * half_cols, 128), half_cols)
        heads = pl.ds(half * half_heads, half_heads)
        rows_in = normed[...]
        for i, (w, rows) in enumerate(((wq, q_rows), (wk, k_rows), (wv, v_rows))):
            if turn == 0:
                loads[i].wait()
            send[heads, rows, :] = by_head(mm(rows_in, w[:, cols], ((1,), (0,))))
        if turn == 0:
            loads[3].wait()
            loads[4].wait()
        gate_in = by_head(mm(rows_in, wg[:, cols], ((1,), (0,))))
        mixed = mm(wo[cols, :], dout_ref[...], ((1,), (1,))).astype(BF16)
        mixed = mixed.reshape(half_heads, DH, PAIR)
        gin[heads] = gate_in
        dmix[heads] = mixed
        gate = jax.nn.sigmoid(gate_in.astype(F32))
        send[heads, g_rows, :] = (mixed.astype(F32) * gate).astype(BF16)
        if turn == 0:
            pl.semaphore_wait(barrier, H + S - 2)
            own_copy.start()
        for off in offsets:
            t = wrap(h + off, H)

            @pl.when(t // half_heads == half)
            def _(t=t):
                forward_copy(t).start()

    crops = lengths_ref.shape[0]
    row = lax.broadcasted_iota(jnp.int32, (crops, PAIR), 0)
    lane = lax.broadcasted_iota(jnp.int32, (crops, PAIR), 1)
    low = jnp.zeros((crops, PAIR), jnp.int32)
    high = jnp.zeros((crops, PAIR), jnp.int32)
    total = jnp.int32(0)
    for c in range(crops):
        low = jnp.where(row == c, total, low)
        total = total + lengths_ref[c]
        high = jnp.where(row == c, total, high)
    for j in range(H + 1):
        pos = (s * H + j - 1) * PAIR + lane
        inside = (pos >= low) & (pos < high)
        hotq[j] = jnp.where(inside, 1.0, 0.0).astype(BF16)
        hotk[j] = jnp.where(inside, 0.0, UNSEEN).astype(BF16)

    def clear(n, carry):
        chain[n] = jnp.zeros((BLOCK, PAIR), F32)
        return carry

    lax.fori_loop(0, 2 * H, clear, 0)

    @pl.when(s == 0)
    def _():
        recv[0] = jnp.zeros((4 * DH, PAIR), BF16)

    key_edge = pltpu.make_async_remote_copy(
        recv.at[H, kv_rows, last_block], recv.at[0, kv_rows, last_block],
        e_send.at[0], e_recv.at[0],
        device_id=(wrap(s + 1, S), h), device_id_type=MESH,
    )
    grad_edge = pltpu.make_async_remote_copy(
        edge_out, edge_in, e_send.at[1], e_recv.at[1],
        device_id=(wrap(s + S - 1, S), h), device_id_type=MESH,
    )

    def back_copy(t):
        return pltpu.make_async_remote_copy(
            res.at[t], got.at[h], b_send.at[t], b_recv.at[h],
            device_id=(s, t), device_id_type=MESH,
        )

    def back_arrival(j):
        return pltpu.make_async_remote_copy(
            res.at[j], got.at[j], b_send.at[j], b_recv.at[j],
            device_id=(s, j), device_id_type=MESH,
        )

    own_back = pltpu.make_async_copy(res.at[h], got.at[h], b_recv.at[h])

    def finish(f):
        later = nxt[f + 1]
        total = own[f]
        res[f, pl.ds(2 * DH, 2 * DH), pl.ds(0, BLOCK)] = total[:, :BLOCK].astype(BF16)
        res[f, pl.ds(2 * DH, 2 * DH), last_block] = (total[:, BLOCK:] + later).astype(BF16)

        @pl.when(f == h)
        def _():
            own_back.start()

        @pl.when(f != h)
        def _():
            back_copy(f).start()

    own_copy.wait()

    @pl.when((h == H - 1) & (s < S - 1))
    def _():
        key_edge.start()

    def attend(j, b, slot):
        n = 2 * j + b
        lanes = pl.ds(b * BLOCK, BLOCK)
        q = recv[j + 1, q_rows, lanes]
        g = recv[j + 1, g_rows, lanes]
        if b == 0:
            k = jnp.concatenate([recv[j, k_rows, last_block], recv[j + 1, k_rows, lanes]], axis=1)
            v = jnp.concatenate([recv[j, v_rows, last_block], recv[j + 1, v_rows, lanes]], axis=1)
            hot = jnp.concatenate([hotk[j, :, last_block], hotk[j + 1, :, lanes]], axis=1)
        else:
            k = recv[j + 1, k_rows, :]
            v = recv[j + 1, v_rows, :]
            hot = hotk[j + 1]
        q_all = jnp.concatenate([q, hotq[j + 1, :, lanes]], axis=0)
        k_all = jnp.concatenate([k, hot], axis=0)
        scores = mm(q_all, k_all, ((0,), (0,))) * scale + bias_ref[tiles_ref[n]].astype(F32)
        weights = jnp.exp(scores - jnp.max(scores, axis=1, keepdims=True))
        probs = weights * (1.0 / jnp.sum(weights, axis=1, keepdims=True))
        probs_low = probs.astype(BF16)
        d_probs = mm(g, v, ((0,), (0,)))
        weighted = probs * d_probs
        d_scores = weighted - probs * jnp.sum(weighted, axis=1, keepdims=True)
        d_low = d_scores.astype(BF16)
        res[j, pl.ds(0, DH), lanes] = mm(v, probs_low, ((1,), (1,))).astype(BF16)
        res[j, pl.ds(DH, DH), lanes] = (mm(k, d_low, ((1,), (1,))) * scale).astype(BF16)
        before = chain_ref[n]
        kept = jnp.where(before >= 0, chain[jnp.maximum(before, 0)], 0.0)
        chain[slot] = kept + d_scores
        d_k = mm(q, d_low, ((1,), (0,))) * scale
        d_v = mm(g, probs_low, ((1,), (0,)))
        return d_k, d_v

    def step(i, carry):
        up = lax.rem(i, 2) == 0
        far = i // 2
        j = wrap(h + jnp.where(up, 1 + far, -far), H)
        arrived = jnp.where(up, j, wrap(j + H - 1, H))

        @pl.when(i < H - 1)
        def _():
            forward_arrival(arrived).wait_recv()

            @pl.when((arrived == H - 1) & (s < S - 1))
            def _():
                key_edge.start()

        @pl.when((j == 0) & (s > 0))
        def _():
            key_edge.wait_recv()

        first_k, first_v = attend(j, 0, 2 * i)
        second_k, second_v = attend(j, 1, 2 * i + 1)
        nxt[j, pl.ds(0, DH), :] = first_k[:, :BLOCK]
        nxt[j, pl.ds(DH, DH), :] = first_v[:, :BLOCK]
        own[j, pl.ds(0, DH), pl.ds(0, BLOCK)] = first_k[:, BLOCK:] + second_k[:, :BLOCK]
        own[j, pl.ds(DH, DH), pl.ds(0, BLOCK)] = first_v[:, BLOCK:] + second_v[:, :BLOCK]
        own[j, pl.ds(0, DH), last_block] = second_k[:, BLOCK:]
        own[j, pl.ds(DH, DH), last_block] = second_v[:, BLOCK:]

        @pl.when((j == 0) & (s > 0))
        def _():
            edge_out[...] = nxt[0].astype(BF16)
            grad_edge.start()

        f = jnp.where(up, wrap(j + H - 1, H), j)

        @pl.when((i > 0) & (f != H - 1))
        def _():
            finish(f)

        return carry

    lax.fori_loop(0, H, step, 0)

    def part_copy(t):
        return pltpu.make_async_remote_copy(
            parts.at[t], parts_in.at[s], r_send.at[t], r_recv.at[s],
            device_id=(t, h), device_id_type=MESH,
        )

    def part_arrival(j):
        return pltpu.make_async_remote_copy(
            parts.at[j], parts_in.at[j], r_send.at[j], r_recv.at[j],
            device_id=(j, h), device_id_type=MESH,
        )

    own_part = pltpu.make_async_copy(parts.at[s], parts_in.at[s], r_recv.at[s])

    def part(o, carry):
        t = wrap(s + o, S)
        at = last_ref[t]
        parts[t] = jnp.where(at >= 0, chain[jnp.maximum(at, 0)], 0.0).astype(BF16)

        @pl.when(t == s)
        def _():
            own_part.start()

        @pl.when(t != s)
        def _():
            part_copy(t).start()

        return carry

    lax.fori_loop(1, S + 1, part, 0)

    opposite = wrap(h + H // 2, H)

    @pl.when(opposite != H - 1)
    def _():
        finish(opposite)

    @pl.when(s < S - 1)
    def _():
        grad_edge.wait_recv()
        nxt[H] = edge_in[...].astype(F32)

    @pl.when(s == S - 1)
    def _():
        nxt[H] = jnp.zeros((2 * DH, BLOCK), F32)

    finish(jnp.int32(H - 1))

    own_part.wait()
    for o in range(1, S):
        part_arrival(wrap(s + o, S)).wait_recv()
    half_block = BLOCK // 2
    for piece in range(2):
        rows = pl.ds(piece * half_block, half_block)
        sums = parts_in[0, rows, :].astype(F32)
        for j in range(1, S):
            sums = sums + parts_in[j, rows, :].astype(F32)
        summed[rows, :] = sums.astype(BF16)

    def sum_copy(t):
        return pltpu.make_async_remote_copy(
            summed, dbias_ref.at[s], a_send.at[t], a_recv.at[s],
            device_id=(t, h), device_id_type=MESH,
        )

    def sum_arrival(j):
        return pltpu.make_async_remote_copy(
            summed, dbias_ref.at[j], a_send.at[j], a_recv.at[j],
            device_id=(j, h), device_id_type=MESH,
        )

    own_sum = pltpu.make_async_copy(summed, dbias_ref.at[s], a_recv.at[s])
    own_sum.start()
    for o in range(1, S):
        sum_copy(wrap(s + o, S)).start()

    own_back.wait()
    for o in range(1, H):
        back_arrival(wrap(h + o, H)).wait_recv()
    gate = jax.nn.sigmoid(gin[...].astype(F32))
    attended = got[:, pl.ds(0, DH), :].astype(F32)
    d_gate = (dmix[...].astype(F32) * attended * gate * (1.0 - gate)).astype(BF16).reshape(D, PAIR)
    got[:, pl.ds(0, DH), :] = d_gate.reshape(H, DH, PAIR)
    chunk = 256

    def product(m, carry):
        rows = pl.ds(pl.multiple_of(m * chunk, chunk), chunk)
        acc = jnp.zeros((chunk, PAIR), F32)
        for i, w in enumerate((wg, wq, wk, wv)):
            grads = got[:, pl.ds(i * DH, DH), :].reshape(D, PAIR)
            acc = acc + mm(w[rows, :], grads, ((1,), (0,)))
        dnorm[rows, :] = acc
        return carry

    lax.fori_loop(0, D // chunk, product, 0)
    for piece in range(2):
        rows = pl.ds(piece * BLOCK, BLOCK)
        g = dnorm[:, rows].T * gain
        xhat = scaled[rows, :]
        centre = jnp.mean(g, axis=1, keepdims=True)
        along = jnp.mean(g * xhat, axis=1, keepdims=True)
        dact_ref[rows, :] = (inverse[rows, :1] * (g - centre - xhat * along)).astype(BF16)

    own_sum.wait()
    for o in range(1, S):
        sum_arrival(wrap(s + o, S)).wait_recv()

    for o in range(1, H):
        t = wrap(h + o, H)
        forward_copy(t).wait_send()
        back_copy(t).wait_send()
    for o in range(1, S):
        t = wrap(s + o, S)
        part_copy(t).wait_send()
        sum_copy(t).wait_send()

    @pl.when(s < S - 1)
    def _():
        key_edge.wait_send()

    @pl.when(s > 0)
    def _():
        grad_edge.wait_send()


def shards(H, S, activations, ln_gain, w_query, w_key, w_value, w_gate, w_out, bias_tiles,
           crop_lengths, tile_index, d_out):
    rows, D = activations.shape
    DH = D // H
    tiles = bias_tiles.shape[0]
    crops = crop_lengths.shape[0]
    h = lax.axis_index("head").astype(jnp.int32)
    n = jnp.arange(2 * H, dtype=jnp.int32)
    above = jnp.remainder(n // 2 - h, H)
    below = jnp.remainder(h - n // 2, H)
    turn = jnp.where((above >= 1) & (above <= H // 2), 2 * (above - 1), 2 * below + 1)
    slot = 2 * turn + n % 2
    same = tile_index[:, None] == tile_index[None, :]
    chain = jnp.max(jnp.where(same & (slot[None, :] < slot[:, None]), slot[None, :], -1), axis=1)
    here = jnp.arange(tiles, dtype=jnp.int32)[:, None] == tile_index[None, :]
    last = jnp.max(jnp.where(here, slot[None, :], -1), axis=1)

    vmem = pl.BlockSpec(memory_space=pltpu.VMEM)
    smem = pl.BlockSpec(memory_space=pltpu.SMEM)
    hbm = pl.BlockSpec(memory_space=pl.ANY)
    dma = pltpu.SemaphoreType.DMA
    d_act, d_bias = pl.pallas_call(
        functools.partial(kernel, H, S, DH),
        out_shape=(
            jax.ShapeDtypeStruct((rows, D), BF16),
            jax.ShapeDtypeStruct((tiles, BLOCK, PAIR), BF16),
        ),
        in_specs=[vmem, vmem, vmem, hbm, hbm, hbm, hbm, hbm, vmem, smem, smem, smem, smem],
        out_specs=(vmem, vmem),
        scratch_shapes=[
            *[pltpu.VMEM((D, D), BF16) for _ in range(5)],
            pltpu.VMEM((rows, D), BF16),
            pltpu.VMEM((rows, D), F32),
            pltpu.VMEM((rows, 128), F32),
            pltpu.VMEM((H, DH, PAIR), BF16),
            pltpu.VMEM((H, DH, PAIR), BF16),
            pltpu.VMEM((H, 4 * DH, PAIR), BF16),
            pltpu.VMEM((H + 1, 4 * DH, PAIR), BF16),
            pltpu.VMEM((H, 4 * DH, PAIR), BF16),
            pltpu.VMEM((H, 4 * DH, PAIR), BF16),
            pltpu.VMEM((H, 2 * DH, PAIR), F32),
            pltpu.VMEM((H + 1, 2 * DH, BLOCK), F32),
            pltpu.VMEM((2 * H, BLOCK, PAIR), F32),
            pltpu.VMEM((H + 1, crops, PAIR), BF16),
            pltpu.VMEM((H + 1, crops, PAIR), BF16),
            pltpu.VMEM((2 * DH, BLOCK), BF16),
            pltpu.VMEM((2 * DH, BLOCK), BF16),
            pltpu.VMEM((tiles, BLOCK, PAIR), BF16),
            pltpu.VMEM((tiles, BLOCK, PAIR), BF16),
            pltpu.VMEM((BLOCK, PAIR), BF16),
            pltpu.VMEM((D, PAIR), F32),
            dma((5,)),
            *[dma((H,)) for _ in range(4)],
            *[dma((S,)) for _ in range(4)],
            dma((2,)),
            dma((2,)),
        ],
        compiler_params=pltpu.CompilerParams(
            collective_id=0, has_side_effects=True, vmem_limit_bytes=50 * 2**20
        ),
    )(
        activations, ln_gain.reshape(1, D), d_out, w_query, w_key, w_value, w_gate, w_out,
        bias_tiles.reshape(tiles, BLOCK, PAIR), crop_lengths, tile_index, chain, last,
    )
    return d_act, d_bias.astype(F32).reshape(tiles, 1, BLOCK, PAIR)


def solution(mesh):
    return jax.shard_map(
        functools.partial(shards, mesh.shape["head"], mesh.shape["seq"]),
        mesh=mesh,
        in_specs=(
            P(("seq", "head"), None),
            P(),
            P(),
            P(),
            P(),
            P(),
            P(),
            P(None, "head", None, None),
            P(),
            P("seq"),
            P(("seq", "head"), None),
        ),
        out_specs=(P(("seq", "head"), None), P(None, "head", None, None)),
        check_vma=False,
    )
```

```python
import functools
import math

import jax
import jax.numpy as jnp
from jax import lax
from jax.experimental import pallas as pl
from jax.experimental.pallas import tpu as pltpu
from jax.sharding import PartitionSpec as P

MESH = pl.DeviceIdType.MESH
F32 = jnp.float32
BF16 = jnp.bfloat16
EPS = 1e-05
UNSEEN = -1e30
BLOCK = 128
PAIR = 2 * BLOCK


def mm(a, b, dims):
    return lax.dot_general(a, b, (dims, ((), ())), preferred_element_type=F32)


def kernel(
    H, S, DH,
    act_hbm, gain_ref, dout_hbm, wq_hbm, wk_hbm, wv_hbm, wg_hbm, wo_hbm, bias_hbm,
    lengths_ref, tiles_ref,
    dact_ref, dbias_ref,
    act, dout, bias, far_bias, order, wq, wk, wv, wg, wo, normed, scaled, inverse, gin, dmix,
    send, recv, res, got, own, nxt, chain, hotq, hotk, edge_out, edge_in,
    parts, first_a, first_b, mid_a, mid_b, second_a, second_b, crossed, dnorm, gated,
    w_sem, f_send, f_recv, b_send, b_recv, k_send, k_recv, e_send, e_recv, c_send, c_recv,
    g_send, g_recv, r_send, r_recv, a_send, a_recv,
):
    s, h = lax.axis_index("seq"), lax.axis_index("head")
    side = math.isqrt(S)
    planes = H // 2
    sx, sy = s // side, lax.rem(s, side)
    z, c = h // 2, lax.rem(h, 2)
    D = H * DH
    half_heads = H // 2
    half_cols = half_heads * DH
    scale = 1.0 / math.sqrt(DH)
    q_rows, k_rows, v_rows, g_rows = (pl.ds(i * DH, DH) for i in range(4))
    kv_rows = pl.ds(DH, 2 * DH)
    last_block = pl.ds(BLOCK, BLOCK)
    upper, lower = pl.ds(0, BLOCK // 2), pl.ds(BLOCK // 2, BLOCK // 2)
    near, far = 5, 3
    starts = {near: 0, far: 2 * near + 1}
    total_slots = 2 * near + 2 * far + 2
    wraps = {near: total_slots, far: total_slots + 1}
    nxt_wraps = {near: total_slots + 1, far: total_slots + 2}

    def wrap(i, n):
        return lax.rem(i + n, n)

    other = wrap(z + planes // 2, planes)
    far_head = 2 * other + c
    heads_of = {near: h, far: far_head}

    def remote(src, dst, a, b, device):
        return pltpu.make_async_remote_copy(
            src, dst, a, b, device_id=device, device_id_type=MESH
        )

    mine = pl.ds(pl.multiple_of(h // half_heads * half_cols, 128), half_cols)
    rest = pl.ds(pl.multiple_of((1 - h // half_heads) * half_cols, 128), half_cols)
    loads = [pltpu.make_async_copy(act_hbm, act, w_sem.at[0])]
    for turn, cols in enumerate((mine, rest)):
        for i, (a, b) in enumerate(((wq_hbm, wq), (wk_hbm, wk), (wv_hbm, wv), (wg_hbm, wg))):
            loads.append(
                pltpu.make_async_copy(a.at[:, cols], b.at[:, cols], w_sem.at[1 + 5 * turn + i])
            )
        loads.append(
            pltpu.make_async_copy(wo_hbm.at[cols, :], wo.at[cols, :], w_sem.at[5 + 5 * turn])
        )
    dout_load = pltpu.make_async_copy(dout_hbm, dout, w_sem.at[11])
    bias_load = pltpu.make_async_copy(bias_hbm, bias, w_sem.at[12])
    for load in loads[:6]:
        load.start()
    dout_load.start()
    for load in loads[6:]:
        load.start()
    bias_load.start()

    barrier = pltpu.get_barrier_semaphore()

    def greet(device):
        pl.semaphore_signal(barrier, inc=1, device_id=device, device_id_type=MESH)

    for o in range(1, H):
        greet((s, wrap(h + o, H)))
    for o in range(1, side):
        greet((wrap(sx + o, side) * side + sy, h))
        greet((sx * side + wrap(sy + o, side), h))
    greet((wrap(s + 1, S), h))
    greet((wrap(s + S - 1, S), h))
    at_end = (z == planes - 1) & (c == 1)
    begins = (z == 1) | (z == 2)

    @pl.when(at_end)
    def _():
        for zo in (1, 2):
            for ch in range(2):
                greet((wrap(s + 1, S), 2 * zo + ch))

    @pl.when(begins)
    def _():
        greet((wrap(s + S - 1, S), H - 1))
        greet((wrap(s + S - 1, S), far_head))

    ends = (z == 1 + planes // 2) | (z == 2 + planes // 2)

    @pl.when(ends)
    def _():
        greet((wrap(s + 1, S), far_head))

    greeted = (
        H - 1 + 2 * (side - 1) + 2
        + jnp.where(at_end, 4, 0) + jnp.where(begins, 2, 0) + jnp.where(ends, 1, 0)
    )

    gain = gain_ref[...].astype(F32).reshape(1, D)
    loads[0].wait()
    x = act[...].astype(F32)
    centred = x - jnp.mean(x, axis=1, keepdims=True)
    inv = lax.rsqrt(jnp.mean(centred * centred, axis=1, keepdims=True) + EPS)
    xhat = centred * inv
    scaled[...] = xhat
    inverse[...] = jnp.broadcast_to(inv, inverse.shape)
    normed[...] = (xhat * gain).astype(BF16)

    def target(d):
        if d in (0, 1, 2, planes - 2, planes - 1):
            return d, starts[near] + 1 + 2 * ((near // 2 - d) % planes)
        return (d + planes // 2) % planes, starts[far] + 1 + 2 * ((far // 2 - d - planes // 2) % planes)

    def forward_copy(d, ch):
        up, place = target(d)
        head = 2 * wrap(z + d, planes) + ch
        return remote(
            send.at[head], recv.at[place + c], f_send.at[2 * d + ch], f_recv.at[place + c],
            (s, 2 * wrap(z + up, planes) + ch),
        )

    def own_copy(d):
        place = target(d)[1] + c
        head = 2 * wrap(z + d, planes) + c
        return pltpu.make_async_copy(send.at[head], recv.at[place], f_recv.at[place])

    def arrival(place):
        return pltpu.make_async_copy(recv.at[place], recv.at[place], f_recv.at[place])

    close = [(d, ch) for d in (0, 1, planes - 1, 4, 5, 3) for ch in range(2)]
    distant = [(d, ch) for d in (2, planes - 2) for ch in range(2)]
    sends = close + distant

    def send_some(which, half):
        for d, ch in which:
            head = 2 * wrap(z + d, planes) + ch
            now = True if half is None else head // half_heads == half
            if d in (0, planes // 2):
                now = now & (c != ch)
            if now is True:
                forward_copy(d, ch).start()
            else:
                @pl.when(now)
                def _(d=d, ch=ch):
                    forward_copy(d, ch).start()

    def by_head(product):
        return product.T.astype(BF16).reshape(half_heads, DH, PAIR)

    cross_bias = remote(
        bias_hbm.at[s], far_bias.at[sx, sy], c_send.at[0], c_recv.at[0], (s, far_head)
    )
    my_half = h // half_heads
    for turn in range(2):
        half = my_half if turn == 0 else 1 - my_half
        cols = mine if turn == 0 else rest
        heads = pl.ds(half * half_heads, half_heads)
        rows_in = normed[...]
        for i, (w, rows) in enumerate(((wq, q_rows), (wk, k_rows), (wv, v_rows))):
            loads[1 + 5 * turn + i].wait()
            send[heads, rows, :] = by_head(mm(rows_in, w[:, cols], ((1,), (0,))))
        for load in loads[4 + 5 * turn:6 + 5 * turn]:
            load.wait()
        if turn == 0:
            dout_load.wait()
        gate_in = by_head(mm(rows_in, wg[:, cols], ((1,), (0,))))
        mixed = mm(wo[cols, :], dout[...], ((1,), (1,))).astype(BF16)
        mixed = mixed.reshape(half_heads, DH, PAIR)
        gin[heads] = gate_in
        dmix[heads] = mixed
        gate = jax.nn.sigmoid(gate_in.astype(F32))
        send[heads, g_rows, :] = (mixed.astype(F32) * gate).astype(BF16)
        if turn == 0:
            pl.semaphore_wait(barrier, greeted)
            cross_bias.start()
            own_copy(0).start()
        else:
            own_copy(planes // 2).start()
        send_some(close, half)

    def key_start(run, ch):
        up = run // 2 + 1
        zo = wrap(z + up, planes)
        head = 2 * (zo if run == near else wrap(zo + planes // 2, planes)) + ch
        group = wrap(s + jnp.where(z == planes - 1, 1, 0), S)
        i = 0 if run == near else 1
        return remote(
            send.at[head, kv_rows, last_block], recv.at[starts[run], kv_rows, last_block],
            k_send.at[2 * i + ch], k_recv.at[i], (group, 2 * zo + ch),
        )

    gives_start = (c == 1) & ((z < planes - 1) | (s < S - 1))

    @pl.when(gives_start)
    def _():
        for ch in range(2):
            key_start(far, ch).start()

    send_some(distant, None)

    @pl.when(gives_start)
    def _():
        for ch in range(2):
            key_start(near, ch).start()

    crops = lengths_ref.shape[0]
    row = lax.broadcasted_iota(jnp.int32, (crops, PAIR), 0)
    lane = lax.broadcasted_iota(jnp.int32, (crops, PAIR), 1)
    low = jnp.zeros((crops, PAIR), jnp.int32)
    high = jnp.zeros((crops, PAIR), jnp.int32)
    total = jnp.int32(0)
    for crop in range(crops):
        low = jnp.where(row == crop, total, low)
        total = total + lengths_ref[crop]
        high = jnp.where(row == crop, total, high)
    for j in range(H + 1):
        pos = (s * H + j - 1) * PAIR + lane
        inside = (pos >= low) & (pos < high)
        hotq[j] = jnp.where(inside, 1.0, 0.0).astype(BF16)
        hotk[j] = jnp.where(inside, 0.0, UNSEEN).astype(BF16)

    def first_pair(run):
        return 2 * wrap(z - run // 2, planes)

    order_at = {near: 0, far: 4 * near}
    for run in (near, far):
        for i in range(2 * run):
            p = run + i // 2 if i % 2 == 0 else run - 1 - i // 2
            j = wrap(first_pair(run) + p, H)
            for b in range(2):
                order[order_at[run] + 2 * i + b] = tiles_ref[2 * j + b]

    def latest(run, tile, before):
        found = jnp.int32(-1)
        for slot in range(order_at[run], order_at[run] + 4 * run):
            found = jnp.where((order[slot] == tile) & (slot < before), slot, found)
        return found

    def clear(n, carry):
        chain[n] = jnp.zeros((BLOCK, PAIR), F32)
        return carry

    lax.fori_loop(0, 2 * H, clear, 0)

    edge_ids = {near: 0, far: 1}

    def has_start(run):
        return (s > 0) | (first_pair(run) != 0)

    def ends_group(run):
        return wrap(first_pair(run) + 2 * run - 1, H) == H - 1

    def has_end(run):
        return (s < S - 1) | jnp.logical_not(ends_group(run))

    def crosses(run):
        return (first_pair(run) != 0) & (first_pair(run) + 2 * run > H)

    for run in (near, far):
        @pl.when(jnp.logical_not(has_start(run)))
        def _(run=run):
            recv[starts[run]] = jnp.zeros((4 * DH, PAIR), BF16)

        @pl.when(crosses(run) & (s == 0))
        def _(run=run):
            recv[wraps[run]] = jnp.zeros((4 * DH, PAIR), BF16)

        @pl.when(jnp.logical_not(has_end(run)))
        def _(run=run):
            nxt[starts[run] + 2 * run + 1] = jnp.zeros((2 * DH, BLOCK), F32)

        @pl.when(crosses(run) & (s == S - 1))
        def _(run=run):
            nxt[nxt_wraps[run]] = jnp.zeros((2 * DH, BLOCK), F32)

    def key_wrap(run):
        at = starts[run] + 1 + wrap(H - 1 - first_pair(run), H)
        i = edge_ids[run]
        return remote(
            recv.at[at, kv_rows, last_block], recv.at[wraps[run], kv_rows, last_block],
            k_send.at[4 + i], k_recv.at[2 + i], (wrap(s + 1, S), h),
        )

    def grad_wrap(run):
        i = edge_ids[run]
        return remote(
            edge_out.at[2 + i], edge_in.at[2 + i], e_send.at[2 + i], e_recv.at[2 + i],
            (wrap(s + S - 1, S), h),
        )

    def grad_start(run):
        i = edge_ids[run]
        group = wrap(s - jnp.where(first_pair(run) == 0, 1, 0), S)
        return remote(
            edge_out.at[i], edge_in.at[1 - i], e_send.at[i], e_recv.at[1 - i], (group, far_head)
        )

    def edge_arrival(i):
        return pltpu.make_async_copy(edge_in.at[i], edge_in.at[i], e_recv.at[i])

    def key_arrival(place, i):
        part = recv.at[place, kv_rows, last_block]
        return pltpu.make_async_copy(part, part, k_recv.at[i])

    def back_copy(run, p):
        place = starts[run] + 1 + p
        return remote(
            res.at[place], got.at[heads_of[run]], b_send.at[place], b_recv.at[heads_of[run]],
            (s, wrap(first_pair(run) + p, H)),
        )

    def own_back(run):
        place = starts[run] + 1 + run - 1 + c
        return pltpu.make_async_copy(res.at[place], got.at[heads_of[run]], b_recv.at[heads_of[run]])

    def back_arrival(head):
        return pltpu.make_async_copy(got.at[head], got.at[head], b_recv.at[head])

    def finish(run, p, after):
        place = starts[run] + 1 + p
        later = nxt[after]
        sums = own[place]
        res[place, pl.ds(2 * DH, 2 * DH), pl.ds(0, BLOCK)] = sums[:, :BLOCK].astype(BF16)
        res[place, pl.ds(2 * DH, 2 * DH), last_block] = (sums[:, BLOCK:] + later).astype(BF16)
        mine_too = p == run - 1 + c

        @pl.when(mine_too)
        def _():
            own_back(run).start()

        @pl.when(jnp.logical_not(mine_too))
        def _():
            back_copy(run, p).start()

    def attend(tiles, place, before_place, j, b, slot, before):
        lanes = pl.ds(b * BLOCK, BLOCK)
        q = recv[place, q_rows, lanes]
        g = recv[place, g_rows, lanes]
        if b == 0:
            k = jnp.concatenate(
                [recv[before_place, k_rows, last_block], recv[place, k_rows, lanes]], axis=1
            )
            v = jnp.concatenate(
                [recv[before_place, v_rows, last_block], recv[place, v_rows, lanes]], axis=1
            )
            hot = jnp.concatenate([hotk[j, :, last_block], hotk[j + 1, :, lanes]], axis=1)
        else:
            k = recv[place, k_rows, :]
            v = recv[place, v_rows, :]
            hot = hotk[j + 1]
        q_all = jnp.concatenate([q, hotq[j + 1, :, lanes]], axis=0)
        k_all = jnp.concatenate([k, hot], axis=0)
        scores = mm(q_all, k_all, ((0,), (0,))) * scale + tiles(order[slot]).astype(F32)
        weights = jnp.exp(scores - jnp.max(scores, axis=1, keepdims=True))
        probs = weights * (1.0 / jnp.sum(weights, axis=1, keepdims=True))
        probs_low = probs.astype(BF16)
        d_probs = mm(g, v, ((0,), (0,)))
        weighted = probs * d_probs
        d_scores = weighted - probs * jnp.sum(weighted, axis=1, keepdims=True)
        d_low = d_scores.astype(BF16)
        res[place, pl.ds(0, DH), lanes] = mm(v, probs_low, ((1,), (1,))).astype(BF16)
        res[place, pl.ds(DH, DH), lanes] = (mm(k, d_low, ((1,), (1,))) * scale).astype(BF16)
        kept = jnp.where(before >= 0, chain[jnp.maximum(before, 0)], 0.0)
        chain[slot] = kept + d_scores
        d_k = mm(q, d_low, ((1,), (0,))) * scale
        d_v = mm(g, probs_low, ((1,), (0,)))
        return d_k, d_v

    def work(run, tiles, begin, end, beside):
        base = starts[run] + 1
        e = edge_ids[run]
        wraps_at = wrap(H - first_pair(run), H)

        def step(i, carry):
            up = lax.rem(i, 2) == 0
            p = jnp.where(up, run + i // 2, run - 1 - i // 2)
            j = wrap(first_pair(run) + p, H)
            arrived = jnp.where(up, p, p - 1)
            beside(i)

            @pl.when(arrived >= 0)
            def _():
                @pl.when(i > 0)
                def _():
                    arrival(base + arrived).wait()

                @pl.when(crosses(run) & (s < S - 1) & (arrived == wraps_at - 1))
                def _():
                    key_wrap(run).start()

            @pl.when((arrived < 0) & has_start(run))
            def _():
                key_arrival(starts[run], e).wait()

            inner = crosses(run) & (p == wraps_at)

            @pl.when(inner & (s > 0))
            def _():
                key_arrival(wraps[run], 2 + e).wait()

            place = base + p
            before_place = jnp.where(inner, wraps[run], place - 1)
            slot = order_at[run] + 2 * i
            first_k, first_v = attend(
                tiles, place, before_place, j, 0, slot, latest(run, order[slot], slot)
            )
            second_k, second_v = attend(
                tiles, place, before_place, j, 1, slot + 1,
                latest(run, order[slot + 1], slot + 1),
            )
            nxt[place, pl.ds(0, DH), :] = first_k[:, :BLOCK]
            nxt[place, pl.ds(DH, DH), :] = first_v[:, :BLOCK]
            own[place, pl.ds(0, DH), pl.ds(0, BLOCK)] = first_k[:, BLOCK:] + second_k[:, :BLOCK]
            own[place, pl.ds(DH, DH), pl.ds(0, BLOCK)] = first_v[:, BLOCK:] + second_v[:, :BLOCK]
            own[place, pl.ds(0, DH), last_block] = second_k[:, BLOCK:]
            own[place, pl.ds(DH, DH), last_block] = second_v[:, BLOCK:]

            @pl.when(inner & (s > 0))
            def _():
                edge_out[2 + e] = nxt[place].astype(BF16)
                grad_wrap(run).start()

            @pl.when((p == 0) & has_start(run))
            def _():
                edge_out[e] = nxt[place].astype(BF16)
                grad_start(run).start()

            f = jnp.where(up, p - 1, p)

            @pl.when((i > 0) & jnp.logical_not(crosses(run) & (f == wraps_at - 1)))
            def _():
                finish(run, f, starts[run] + 2 + f)

            return carry

        lax.fori_loop(begin, end, step, 0)

    def passed_over(run):
        e = edge_ids[run]

        @pl.when(crosses(run))
        def _():
            @pl.when(s < S - 1)
            def _():
                edge_arrival(2 + e).wait()
                nxt[nxt_wraps[run]] = edge_in[2 + e].astype(F32)

            finish(run, wrap(H - first_pair(run), H) - 1, nxt_wraps[run])

    def last_of(run):
        e = edge_ids[run]

        @pl.when(has_end(run))
        def _():
            edge_arrival(e).wait()
            nxt[starts[run] + 2 * run + 1] = edge_in[e].astype(F32)

        finish(run, jnp.int32(2 * run - 1), starts[run] + 2 * run + 1)

    def x_of(o):
        return (wrap(sx + o, side) * side + sy, h)

    def y_of(o):
        return (sx * side + wrap(sy + o, side), h)

    def gather_copies(ref, a, b):
        one, two = [], []
        for o in range(1, side):
            one.append(remote(
                ref.at[sx, sy, upper], ref.at[sx, sy, upper], a.at[0, o], b.at[0, o], x_of(o)
            ))
            one.append(remote(
                ref.at[sx, sy, lower], ref.at[sx, sy, lower], a.at[1, o], b.at[1, o], y_of(o)
            ))
            two.append(remote(
                ref.at[:, sy, upper], ref.at[:, sy, upper], a.at[2, o], b.at[2, o], y_of(o)
            ))
            two.append(remote(
                ref.at[sx, :, lower], ref.at[sx, :, lower], a.at[3, o], b.at[3, o], x_of(o)
            ))
        return one, two

    def local(ref, sem):
        return pltpu.make_async_copy(ref, ref, sem)

    def gather_arrivals(ref, b):
        one, two = [], []
        for o in range(1, side):
            fx, fy = wrap(sx - o, side), wrap(sy - o, side)
            one.append(local(ref.at[fx, sy, upper], b.at[0, o]))
            one.append(local(ref.at[sx, fy, lower], b.at[1, o]))
            two.append(local(ref.at[:, fy, upper], b.at[2, o]))
            two.append(local(ref.at[fx, :, lower], b.at[3, o]))
        return one, two

    bias_one, bias_two = gather_copies(far_bias, g_send, g_recv)
    bias_in_one, bias_in_two = gather_arrivals(far_bias, g_recv)

    def bias_steps(i):
        @pl.when(i == 1)
        def _():
            local(far_bias.at[sx, sy], c_recv.at[0]).wait()
            for copy in bias_one:
                copy.start()

        @pl.when(i == 4)
        def _():
            for copy in bias_in_one:
                copy.wait()
            for copy in bias_two:
                copy.start()

    def scatter_one(k):
        copies = []
        for o in range(1, side):
            copies.append(remote(
                parts.at[k, wrap(sx + o, side), :, upper], first_a.at[k, o - 1],
                r_send.at[k, 0, o], r_recv.at[k, 0, o], x_of(o),
            ))
            copies.append(remote(
                parts.at[k, :, wrap(sy + o, side), lower], first_b.at[k, o - 1],
                r_send.at[k, 1, o], r_recv.at[k, 1, o], y_of(o),
            ))
        return copies

    def scatter_two(k):
        copies = []
        for o in range(1, side):
            copies.append(remote(
                mid_a.at[k, wrap(sy + o, side)], second_a.at[k, o - 1],
                r_send.at[k, 2, o], r_recv.at[k, 2, o], y_of(o),
            ))
            copies.append(remote(
                mid_b.at[k, wrap(sx + o, side)], second_b.at[k, o - 1],
                r_send.at[k, 3, o], r_recv.at[k, 3, o], x_of(o),
            ))
        return copies

    def begin_sums(run):
        k = edge_ids[run]

        def part(t, carry):
            at = latest(run, t, 2 * H)
            parts[k, t // side, lax.rem(t, side)] = jnp.where(
                at >= 0, chain[jnp.maximum(at, 0)], 0.0
            ).astype(BF16)
            return carry

        lax.fori_loop(0, S, part, 0)
        for copy in scatter_one(k):
            copy.start()

    def middle_sums(run):
        k = edge_ids[run]
        for o in range(1, side):
            local(first_a.at[k, o - 1], r_recv.at[k, 0, o]).wait()
            local(first_b.at[k, o - 1], r_recv.at[k, 1, o]).wait()
        for i in range(side):
            a = parts[k, sx, i, upper].astype(F32)
            b = parts[k, i, sy, lower].astype(F32)
            for o in range(side - 1):
                a = a + first_a[k, o, i].astype(F32)
                b = b + first_b[k, o, i].astype(F32)
            mid_a[k, i] = a.astype(BF16)
            mid_b[k, i] = b.astype(BF16)
        for copy in scatter_two(k):
            copy.start()

    def end_sums(run):
        k = edge_ids[run]
        for o in range(1, side):
            local(second_a.at[k, o - 1], r_recv.at[k, 2, o]).wait()
            local(second_b.at[k, o - 1], r_recv.at[k, 3, o]).wait()
        a = mid_a[k, sy].astype(F32)
        b = mid_b[k, sx].astype(F32)
        for o in range(side - 1):
            a = a + second_a[k, o].astype(F32)
            b = b + second_b[k, o].astype(F32)
        return a, b

    own_copy(0).wait()
    arrival(starts[near] + 1 + near - c).wait()
    bias_load.wait()
    work(near, lambda t: bias[t], 0, near, bias_steps)

    own_copy(planes // 2).wait()
    arrival(starts[far] + 1 + far - c).wait()
    for copy in bias_in_two:
        copy.wait()
    work(far, lambda t: far_bias[t // side, lax.rem(t, side)], 0, 2 * far, lambda i: None)
    begin_sums(far)
    passed_over(far)

    def sum_steps(i):
        @pl.when(i == near + 2)
        def _():
            middle_sums(far)

    work(near, lambda t: bias[t], near, 2 * near, sum_steps)
    begin_sums(near)
    far_a, far_b = end_sums(far)
    crossed[0, upper] = far_a.astype(BF16)
    crossed[0, lower] = far_b.astype(BF16)
    cross_sum = remote(
        crossed.at[0], crossed.at[1], c_send.at[1], c_recv.at[1], (s, far_head)
    )
    cross_sum.start()
    passed_over(near)
    last_of(far)
    last_of(near)
    gate = jax.nn.sigmoid(gin[...].astype(F32))
    gated[...] = dmix[...].astype(F32) * gate * (1.0 - gate)
    middle_sums(near)
    own_a, own_b = end_sums(near)
    local(crossed.at[1], c_recv.at[1]).wait()
    dbias_ref[sx, sy, upper] = (own_a + crossed[1, upper].astype(F32)).astype(BF16)
    dbias_ref[sx, sy, lower] = (own_b + crossed[1, lower].astype(F32)).astype(BF16)
    out_one, out_two = gather_copies(dbias_ref, a_send, a_recv)
    in_one, in_two = gather_arrivals(dbias_ref, a_recv)
    for copy in out_one:
        copy.start()
    for copy in in_one:
        copy.wait()
    for copy in out_two:
        copy.start()

    for head in range(H):
        back_arrival(head).wait()
    attended = got[:, pl.ds(0, DH), :].astype(F32)
    got[:, pl.ds(0, DH), :] = (gated[...] * attended).astype(BF16)
    chunk = 256

    def product(m, carry):
        rows = pl.ds(pl.multiple_of(m * chunk, chunk), chunk)
        acc = jnp.zeros((chunk, PAIR), F32)
        for i, w in enumerate((wg, wq, wk, wv)):
            grads = got[:, pl.ds(i * DH, DH), :].reshape(D, PAIR)
            acc = acc + mm(w[rows, :], grads, ((1,), (0,)))
        dnorm[rows, :] = acc
        return carry

    lax.fori_loop(0, D // chunk, product, 0)
    for piece in range(2):
        rows = pl.ds(piece * BLOCK, BLOCK)
        g = dnorm[:, rows].T * gain
        xhat = scaled[rows, :]
        centre = jnp.mean(g, axis=1, keepdims=True)
        along = jnp.mean(g * xhat, axis=1, keepdims=True)
        dact_ref[rows, :] = (inverse[rows, :1] * (g - centre - xhat * along)).astype(BF16)

    for copy in in_two:
        copy.wait()

    for d, ch in sends:
        if d in (0, planes // 2):
            @pl.when(c != ch)
            def _(d=d, ch=ch):
                forward_copy(d, ch).wait_send()
        else:
            forward_copy(d, ch).wait_send()
    cross_bias.wait_send()
    cross_sum.wait_send()
    for copy in bias_one + bias_two + out_one + out_two:
        copy.wait_send()
    for k in range(2):
        for copy in scatter_one(k) + scatter_two(k):
            copy.wait_send()

    @pl.when(gives_start)
    def _():
        for run in (near, far):
            for ch in range(2):
                key_start(run, ch).wait_send()

    for run in (near, far):
        @pl.when(crosses(run) & (s < S - 1))
        def _(run=run):
            key_wrap(run).wait_send()

        @pl.when(crosses(run) & (s > 0))
        def _(run=run):
            grad_wrap(run).wait_send()

        @pl.when(has_start(run))
        def _(run=run):
            grad_start(run).wait_send()

        for p in range(2 * run):
            if p in (run - 1, run):
                @pl.when(p != run - 1 + c)
                def _(run=run, p=p):
                    back_copy(run, p).wait_send()
            else:
                back_copy(run, p).wait_send()


def shards(H, S, activations, ln_gain, w_query, w_key, w_value, w_gate, w_out, bias_tiles,
           crop_lengths, tile_index, d_out):
    rows, D = activations.shape
    DH = D // H
    tiles = bias_tiles.shape[0]
    crops = crop_lengths.shape[0]
    vmem = pl.BlockSpec(memory_space=pltpu.VMEM)
    smem = pl.BlockSpec(memory_space=pltpu.SMEM)
    hbm = pl.BlockSpec(memory_space=pl.ANY)
    dma = pltpu.SemaphoreType.DMA
    side = math.isqrt(S)
    slots = H + 2
    half = BLOCK // 2
    d_act, d_bias = pl.pallas_call(
        functools.partial(kernel, H, S, DH),
        out_shape=(
            jax.ShapeDtypeStruct((rows, D), BF16),
            jax.ShapeDtypeStruct((side, side, BLOCK, PAIR), BF16),
        ),
        in_specs=[hbm, vmem, hbm, hbm, hbm, hbm, hbm, hbm, hbm, smem, smem],
        out_specs=(vmem, vmem),
        scratch_shapes=[
            pltpu.VMEM((rows, D), BF16),
            pltpu.VMEM((rows, D), BF16),
            pltpu.VMEM((tiles, BLOCK, PAIR), BF16),
            pltpu.VMEM((side, side, BLOCK, PAIR), BF16),
            pltpu.SMEM((2 * H,), jnp.int32),
            *[pltpu.VMEM((D, D), BF16) for _ in range(5)],
            pltpu.VMEM((rows, D), BF16),
            pltpu.VMEM((rows, D), F32),
            pltpu.VMEM((rows, 128), F32),
            pltpu.VMEM((H, DH, PAIR), BF16),
            pltpu.VMEM((H, DH, PAIR), BF16),
            pltpu.VMEM((H, 4 * DH, PAIR), BF16),
            pltpu.VMEM((slots + 2, 4 * DH, PAIR), BF16),
            pltpu.VMEM((slots, 4 * DH, PAIR), BF16),
            pltpu.VMEM((H, 4 * DH, PAIR), BF16),
            pltpu.VMEM((slots, 2 * DH, PAIR), F32),
            pltpu.VMEM((slots + 3, 2 * DH, BLOCK), F32),
            pltpu.VMEM((2 * H, BLOCK, PAIR), F32),
            pltpu.VMEM((H + 1, crops, PAIR), BF16),
            pltpu.VMEM((H + 1, crops, PAIR), BF16),
            pltpu.VMEM((4, 2 * DH, BLOCK), BF16),
            pltpu.VMEM((4, 2 * DH, BLOCK), BF16),
            pltpu.VMEM((2, side, side, BLOCK, PAIR), BF16),
            pltpu.VMEM((2, side - 1, side, half, PAIR), BF16),
            pltpu.VMEM((2, side - 1, side, half, PAIR), BF16),
            pltpu.VMEM((2, side, half, PAIR), BF16),
            pltpu.VMEM((2, side, half, PAIR), BF16),
            pltpu.VMEM((2, side - 1, half, PAIR), BF16),
            pltpu.VMEM((2, side - 1, half, PAIR), BF16),
            pltpu.VMEM((2, BLOCK, PAIR), BF16),
            pltpu.VMEM((D, PAIR), F32),
            pltpu.VMEM((H, DH, PAIR), F32),
            dma((13,)),
            dma((H,)), dma((slots,)), dma((slots,)), dma((H,)),
            dma((6,)), dma((4,)), dma((4,)), dma((4,)), dma((2,)), dma((2,)),
            dma((4, side)), dma((4, side)), dma((2, 4, side)), dma((2, 4, side)),
            dma((4, side)), dma((4, side)),
        ],
        compiler_params=pltpu.CompilerParams(
            collective_id=0, has_side_effects=True, vmem_limit_bytes=60 * 2**20
        ),
    )(
        activations, ln_gain, d_out, w_query, w_key, w_value, w_gate, w_out,
        bias_tiles.reshape(tiles, BLOCK, PAIR), crop_lengths, tile_index,
    )
    return d_act, d_bias.astype(F32).reshape(tiles, 1, BLOCK, PAIR)


def solution(mesh):
    return jax.shard_map(
        functools.partial(shards, mesh.shape["head"], mesh.shape["seq"]),
        mesh=mesh,
        in_specs=(
            P(("seq", "head"), None),
            P(),
            P(),
            P(),
            P(),
            P(),
            P(),
            P(None, "head", None, None),
            P(),
            P("seq"),
            P(("seq", "head"), None),
        ),
        out_specs=(P(("seq", "head"), None), P(None, "head", None, None)),
        check_vma=False,
    )
```

```python
import functools
import math

import jax
import jax.numpy as jnp
from jax import lax
from jax.experimental import pallas as pl
from jax.experimental.pallas import tpu as pltpu
from jax.sharding import PartitionSpec as P

MESH = pl.DeviceIdType.MESH
F32 = jnp.float32
BF16 = jnp.bfloat16
EPS = 1e-05
UNSEEN = -1e30
BLOCK = 128
PAIR = 2 * BLOCK


def mm(a, b, dims):
    return lax.dot_general(a, b, (dims, ((), ())), preferred_element_type=F32)


def kernel(
    H, S, DH,
    act_hbm, gain_ref, dout_hbm, wq_hbm, wk_hbm, wv_hbm, wg_hbm, wo_hbm, bias_hbm,
    lengths_ref, tiles_ref,
    dact_ref, dbias_ref,
    act, dout, bias, tile, own_tile, near_bias, far_bias, order, wq, wk, wv, wg, wo, normed, scaled, inverse, gin, dmix,
    send, recv, res, got, own, nxt, chain, hotq, hotk, edge_out, edge_in,
    parts, first_a, first_b, mid_a, mid_b, second_a, second_b, crossed, dnorm, gated,
    w_sem, f_send, f_recv, b_send, b_recv, k_send, k_recv, e_send, e_recv, c_send, c_recv,
    g_send, g_recv, r_send, r_recv, a_send, a_recv,
):
    s, h = lax.axis_index("seq"), lax.axis_index("head")
    side = math.isqrt(S)
    planes = H // 2
    sx, sy = s // side, lax.rem(s, side)
    z, c = h // 2, lax.rem(h, 2)
    D = H * DH
    half_heads = H // 2
    half_cols = half_heads * DH
    scale = 1.0 / math.sqrt(DH)
    q_rows, k_rows, v_rows, g_rows = (pl.ds(i * DH, DH) for i in range(4))
    kv_rows = pl.ds(DH, 2 * DH)
    last_block = pl.ds(BLOCK, BLOCK)
    out_halves = pl.ds(0, BLOCK // 2), pl.ds(BLOCK // 2, BLOCK // 2)
    halves = pl.ds(0, BLOCK), pl.ds(BLOCK, BLOCK)
    upper, lower = halves
    near, far = 5, 3
    starts = {near: 0, far: 2 * near + 1}
    total_slots = 2 * near + 2 * far + 2
    wraps = {near: total_slots, far: total_slots + 1}
    nxt_wraps = {near: total_slots + 1, far: total_slots + 2}

    def wrap(i, n):
        return lax.rem(i + n, n)

    other = wrap(z + planes // 2, planes)
    far_head = 2 * other + c
    heads_of = {near: h, far: far_head}

    def remote(src, dst, a, b, device):
        return pltpu.make_async_remote_copy(
            src, dst, a, b, device_id=device, device_id_type=MESH
        )

    mine = pl.ds(pl.multiple_of(h // half_heads * half_cols, 128), half_cols)
    rest = pl.ds(pl.multiple_of((1 - h // half_heads) * half_cols, 128), half_cols)
    loads = [pltpu.make_async_copy(act_hbm, act, w_sem.at[0])]
    for turn, cols in enumerate((mine, rest)):
        for i, (a, b) in enumerate(((wq_hbm, wq), (wk_hbm, wk), (wv_hbm, wv), (wg_hbm, wg))):
            loads.append(
                pltpu.make_async_copy(a.at[:, cols], b.at[:, cols], w_sem.at[1 + 5 * turn + i])
            )
        loads.append(
            pltpu.make_async_copy(wo_hbm.at[cols, :], wo.at[cols, :], w_sem.at[5 + 5 * turn])
        )
    dout_load = pltpu.make_async_copy(dout_hbm, dout, w_sem.at[11])
    bias_load = pltpu.make_async_copy(bias_hbm, bias, w_sem.at[12])
    tile_load = pltpu.make_async_copy(bias_hbm.at[s], tile, w_sem.at[13])
    for load in loads[:6]:
        load.start()
    tile_load.start()
    dout_load.start()
    for load in loads[6:]:
        load.start()
    bias_load.start()

    barrier = pltpu.get_barrier_semaphore()

    def greet(device):
        pl.semaphore_signal(barrier, inc=1, device_id=device, device_id_type=MESH)

    for o in range(1, H):
        greet((s, wrap(h + o, H)))
    for o in range(1, side):
        greet((wrap(sx + o, side) * side + sy, h))
        greet((sx * side + wrap(sy + o, side), h))
    greet((wrap(s + 1, S), h))
    greet((wrap(s + S - 1, S), h))
    at_end = (z == planes - 1) & (c == 1)
    begins = (z == 1) | (z == 2)

    @pl.when(at_end)
    def _():
        for zo in (1, 2):
            for ch in range(2):
                greet((wrap(s + 1, S), 2 * zo + ch))

    @pl.when(begins)
    def _():
        greet((wrap(s + S - 1, S), H - 1))
        greet((wrap(s + S - 1, S), far_head))

    ends = (z == 1 + planes // 2) | (z == 2 + planes // 2)

    @pl.when(ends)
    def _():
        greet((wrap(s + 1, S), far_head))

    greeted = (
        H - 1 + 2 * (side - 1) + 2
        + jnp.where(at_end, 4, 0) + jnp.where(begins, 2, 0) + jnp.where(ends, 1, 0)
    )

    gain = gain_ref[...].astype(F32).reshape(1, D)
    loads[0].wait()
    x = act[...].astype(F32)
    centred = x - jnp.mean(x, axis=1, keepdims=True)
    inv = lax.rsqrt(jnp.mean(centred * centred, axis=1, keepdims=True) + EPS)
    xhat = centred * inv
    scaled[...] = xhat
    inverse[...] = jnp.broadcast_to(inv, inverse.shape)
    normed[...] = (xhat * gain).astype(BF16)

    def target(d):
        if d in (0, 1, 2, planes - 2, planes - 1):
            return d, starts[near] + 1 + 2 * ((near // 2 - d) % planes)
        return (d + planes // 2) % planes, starts[far] + 1 + 2 * ((far // 2 - d - planes // 2) % planes)

    def forward_copy(d, ch):
        up, place = target(d)
        head = 2 * wrap(z + d, planes) + ch
        return remote(
            send.at[head], recv.at[place + c], f_send.at[2 * d + ch], f_recv.at[place + c],
            (s, 2 * wrap(z + up, planes) + ch),
        )

    def own_copy(d):
        place = target(d)[1] + c
        head = 2 * wrap(z + d, planes) + c
        return pltpu.make_async_copy(send.at[head], recv.at[place], f_recv.at[place])

    def arrival(place):
        return pltpu.make_async_copy(recv.at[place], recv.at[place], f_recv.at[place])

    close = [(d, ch) for d in (0, 1, planes - 1, 4, 5, 3) for ch in range(2)]
    distant = [(d, ch) for d in (2, planes - 2) for ch in range(2)]
    sends = close + distant

    def send_some(which, half):
        for d, ch in which:
            head = 2 * wrap(z + d, planes) + ch
            now = True if half is None else head // half_heads == half
            if d in (0, planes // 2):
                now = now & (c != ch)
            if now is True:
                forward_copy(d, ch).start()
            else:
                @pl.when(now)
                def _(d=d, ch=ch):
                    forward_copy(d, ch).start()

    def by_head(product):
        return product.T.astype(BF16).reshape(half_heads, DH, PAIR)

    cross_bias = remote(
        own_tile, far_bias.at[sx, sy], c_send.at[0], c_recv.at[0], (s, far_head)
    )
    tile_load.wait()
    own_tile[...] = tile[...].astype(F32).T.astype(BF16)
    pl.semaphore_wait(barrier, greeted)
    cross_bias.start()
    my_half = h // half_heads
    for turn in range(2):
        half = my_half if turn == 0 else 1 - my_half
        cols = mine if turn == 0 else rest
        heads = pl.ds(half * half_heads, half_heads)
        rows_in = normed[...]
        for i, (w, rows) in enumerate(((wq, q_rows), (wk, k_rows), (wv, v_rows))):
            loads[1 + 5 * turn + i].wait()
            send[heads, rows, :] = by_head(mm(rows_in, w[:, cols], ((1,), (0,))))
        for load in loads[4 + 5 * turn:6 + 5 * turn]:
            load.wait()
        if turn == 0:
            dout_load.wait()
        gate_in = by_head(mm(rows_in, wg[:, cols], ((1,), (0,))))
        mixed = mm(wo[cols, :], dout[...], ((1,), (1,))).astype(BF16)
        mixed = mixed.reshape(half_heads, DH, PAIR)
        gin[heads] = gate_in
        dmix[heads] = mixed
        gate = jax.nn.sigmoid(gate_in.astype(F32))
        send[heads, g_rows, :] = (mixed.astype(F32) * gate).astype(BF16)
        if turn == 0:
            own_copy(0).start()
        else:
            own_copy(planes // 2).start()
        send_some(close, half)

    def key_start(run, ch):
        up = run // 2 + 1
        zo = wrap(z + up, planes)
        head = 2 * (zo if run == near else wrap(zo + planes // 2, planes)) + ch
        group = wrap(s + jnp.where(z == planes - 1, 1, 0), S)
        i = 0 if run == near else 1
        return remote(
            send.at[head, kv_rows, last_block], recv.at[starts[run], kv_rows, last_block],
            k_send.at[2 * i + ch], k_recv.at[i], (group, 2 * zo + ch),
        )

    gives_start = (c == 1) & ((z < planes - 1) | (s < S - 1))

    @pl.when(gives_start)
    def _():
        for ch in range(2):
            key_start(far, ch).start()

    send_some(distant, None)

    @pl.when(gives_start)
    def _():
        for ch in range(2):
            key_start(near, ch).start()

    crops = lengths_ref.shape[0]
    row = lax.broadcasted_iota(jnp.int32, (crops, PAIR), 0)
    lane = lax.broadcasted_iota(jnp.int32, (crops, PAIR), 1)
    low = jnp.zeros((crops, PAIR), jnp.int32)
    high = jnp.zeros((crops, PAIR), jnp.int32)
    total = jnp.int32(0)
    for crop in range(crops):
        low = jnp.where(row == crop, total, low)
        total = total + lengths_ref[crop]
        high = jnp.where(row == crop, total, high)
    for j in range(H + 1):
        pos = (s * H + j - 1) * PAIR + lane
        inside = (pos >= low) & (pos < high)
        hotq[j] = jnp.where(inside, 1.0, 0.0).astype(BF16)
        hotk[j] = jnp.where(inside, 0.0, UNSEEN).astype(BF16)

    def first_pair(run):
        return 2 * wrap(z - run // 2, planes)

    order_at = {near: 0, far: 4 * near}
    for run in (near, far):
        for i in range(2 * run):
            p = run + i // 2 if i % 2 == 0 else run - 1 - i // 2
            j = wrap(first_pair(run) + p, H)
            for b in range(2):
                order[order_at[run] + 2 * i + b] = tiles_ref[2 * j + b]

    def latest(run, tile, before):
        found = jnp.int32(-1)
        for slot in range(order_at[run], order_at[run] + 4 * run):
            found = jnp.where((order[slot] == tile) & (slot < before), slot, found)
        return found

    def clear(n, carry):
        chain[n] = jnp.zeros((PAIR, BLOCK), F32)
        return carry

    lax.fori_loop(0, 2 * H, clear, 0)

    def turn_tile(n, carry):
        near_bias[n] = bias[n].astype(F32).T.astype(BF16)
        return carry

    bias_load.wait()
    lax.fori_loop(0, bias.shape[0], turn_tile, 0)

    edge_ids = {near: 0, far: 1}

    def has_start(run):
        return (s > 0) | (first_pair(run) != 0)

    def ends_group(run):
        return wrap(first_pair(run) + 2 * run - 1, H) == H - 1

    def has_end(run):
        return (s < S - 1) | jnp.logical_not(ends_group(run))

    def crosses(run):
        return (first_pair(run) != 0) & (first_pair(run) + 2 * run > H)

    for run in (near, far):
        @pl.when(jnp.logical_not(has_start(run)))
        def _(run=run):
            recv[starts[run]] = jnp.zeros((4 * DH, PAIR), BF16)

        @pl.when(crosses(run) & (s == 0))
        def _(run=run):
            recv[wraps[run]] = jnp.zeros((4 * DH, PAIR), BF16)

        @pl.when(jnp.logical_not(has_end(run)))
        def _(run=run):
            nxt[starts[run] + 2 * run + 1] = jnp.zeros((2 * DH, BLOCK), F32)

        @pl.when(crosses(run) & (s == S - 1))
        def _(run=run):
            nxt[nxt_wraps[run]] = jnp.zeros((2 * DH, BLOCK), F32)

    def key_wrap(run):
        at = starts[run] + 1 + wrap(H - 1 - first_pair(run), H)
        i = edge_ids[run]
        return remote(
            recv.at[at, kv_rows, last_block], recv.at[wraps[run], kv_rows, last_block],
            k_send.at[4 + i], k_recv.at[2 + i], (wrap(s + 1, S), h),
        )

    def grad_wrap(run):
        i = edge_ids[run]
        return remote(
            edge_out.at[2 + i], edge_in.at[2 + i], e_send.at[2 + i], e_recv.at[2 + i],
            (wrap(s + S - 1, S), h),
        )

    def grad_start(run):
        i = edge_ids[run]
        group = wrap(s - jnp.where(first_pair(run) == 0, 1, 0), S)
        return remote(
            edge_out.at[i], edge_in.at[1 - i], e_send.at[i], e_recv.at[1 - i], (group, far_head)
        )

    def edge_arrival(i):
        return pltpu.make_async_copy(edge_in.at[i], edge_in.at[i], e_recv.at[i])

    def key_arrival(place, i):
        part = recv.at[place, kv_rows, last_block]
        return pltpu.make_async_copy(part, part, k_recv.at[i])

    def back_copy(run, p):
        place = starts[run] + 1 + p
        return remote(
            res.at[place], got.at[heads_of[run]], b_send.at[place], b_recv.at[heads_of[run]],
            (s, wrap(first_pair(run) + p, H)),
        )

    def own_back(run):
        place = starts[run] + 1 + run - 1 + c
        return pltpu.make_async_copy(res.at[place], got.at[heads_of[run]], b_recv.at[heads_of[run]])

    def back_arrival(head):
        return pltpu.make_async_copy(got.at[head], got.at[head], b_recv.at[head])

    def finish(run, p, after):
        place = starts[run] + 1 + p
        later = nxt[after]
        sums = own[place]
        res[place, pl.ds(2 * DH, 2 * DH), pl.ds(0, BLOCK)] = sums[:, :BLOCK].astype(BF16)
        res[place, pl.ds(2 * DH, 2 * DH), last_block] = (sums[:, BLOCK:] + later).astype(BF16)
        mine_too = p == run - 1 + c

        @pl.when(mine_too)
        def _():
            own_back(run).start()

        @pl.when(jnp.logical_not(mine_too))
        def _():
            back_copy(run, p).start()

    def attend(tiles, place, before_place, j, b, slot, before):
        lanes = pl.ds(b * BLOCK, BLOCK)
        q = recv[place, q_rows, lanes]
        g = recv[place, g_rows, lanes]
        if b == 0:
            k = jnp.concatenate(
                [recv[before_place, k_rows, last_block], recv[place, k_rows, lanes]], axis=1
            )
            v = jnp.concatenate(
                [recv[before_place, v_rows, last_block], recv[place, v_rows, lanes]], axis=1
            )
            hot = jnp.concatenate([hotk[j, :, last_block], hotk[j + 1, :, lanes]], axis=1)
        else:
            k = recv[place, k_rows, :]
            v = recv[place, v_rows, :]
            hot = hotk[j + 1]
        q_all = jnp.concatenate([q, hotq[j + 1, :, lanes]], axis=0)
        k_all = jnp.concatenate([k, hot], axis=0)
        scores = mm(k_all, q_all, ((0,), (0,))) * scale + tiles(order[slot]).astype(F32)
        weights = jnp.exp(scores - jnp.max(scores, axis=0, keepdims=True))
        probs = weights * (1.0 / jnp.sum(weights, axis=0, keepdims=True))
        probs_low = probs.astype(BF16)
        d_probs = mm(v, g, ((0,), (0,)))
        d_scores = probs * (d_probs - jnp.sum(probs * d_probs, axis=0, keepdims=True))
        d_low = d_scores.astype(BF16)
        res[place, pl.ds(0, DH), lanes] = mm(v, probs_low, ((1,), (0,))).astype(BF16)
        res[place, pl.ds(DH, DH), lanes] = (mm(k, d_low, ((1,), (0,))) * scale).astype(BF16)
        kept = jnp.where(before >= 0, chain[jnp.maximum(before, 0)], 0.0)
        chain[slot] = kept + d_scores
        d_k = mm(q, d_low, ((1,), (1,))) * scale
        d_v = mm(g, probs_low, ((1,), (1,)))
        return d_k, d_v

    def work(run, tiles, begin, end, beside):
        base = starts[run] + 1
        e = edge_ids[run]
        wraps_at = wrap(H - first_pair(run), H)

        def step(i, carry):
            up = lax.rem(i, 2) == 0
            p = jnp.where(up, run + i // 2, run - 1 - i // 2)
            j = wrap(first_pair(run) + p, H)
            arrived = jnp.where(up, p, p - 1)
            beside(i)

            @pl.when(arrived >= 0)
            def _():
                @pl.when(i > 0)
                def _():
                    arrival(base + arrived).wait()

                @pl.when(crosses(run) & (s < S - 1) & (arrived == wraps_at - 1))
                def _():
                    key_wrap(run).start()

            @pl.when((arrived < 0) & has_start(run))
            def _():
                key_arrival(starts[run], e).wait()

            inner = crosses(run) & (p == wraps_at)

            @pl.when(inner & (s > 0))
            def _():
                key_arrival(wraps[run], 2 + e).wait()

            place = base + p
            before_place = jnp.where(inner, wraps[run], place - 1)
            slot = order_at[run] + 2 * i
            first_k, first_v = attend(
                tiles, place, before_place, j, 0, slot, latest(run, order[slot], slot)
            )
            second_k, second_v = attend(
                tiles, place, before_place, j, 1, slot + 1,
                latest(run, order[slot + 1], slot + 1),
            )
            nxt[place, pl.ds(0, DH), :] = first_k[:, :BLOCK]
            nxt[place, pl.ds(DH, DH), :] = first_v[:, :BLOCK]
            own[place, pl.ds(0, DH), pl.ds(0, BLOCK)] = first_k[:, BLOCK:] + second_k[:, :BLOCK]
            own[place, pl.ds(DH, DH), pl.ds(0, BLOCK)] = first_v[:, BLOCK:] + second_v[:, :BLOCK]
            own[place, pl.ds(0, DH), last_block] = second_k[:, BLOCK:]
            own[place, pl.ds(DH, DH), last_block] = second_v[:, BLOCK:]

            @pl.when(inner & (s > 0))
            def _():
                edge_out[2 + e] = nxt[place].astype(BF16)
                grad_wrap(run).start()

            @pl.when((p == 0) & has_start(run))
            def _():
                edge_out[e] = nxt[place].astype(BF16)
                grad_start(run).start()

            f = jnp.where(up, p - 1, p)

            @pl.when((i > 0) & jnp.logical_not(crosses(run) & (f == wraps_at - 1)))
            def _():
                finish(run, f, starts[run] + 2 + f)

            return carry

        lax.fori_loop(begin, end, step, 0)

    def passed_over(run):
        e = edge_ids[run]

        @pl.when(crosses(run))
        def _():
            @pl.when(s < S - 1)
            def _():
                edge_arrival(2 + e).wait()
                nxt[nxt_wraps[run]] = edge_in[2 + e].astype(F32)

            finish(run, wrap(H - first_pair(run), H) - 1, nxt_wraps[run])

    def last_of(run):
        e = edge_ids[run]

        @pl.when(has_end(run))
        def _():
            edge_arrival(e).wait()
            nxt[starts[run] + 2 * run + 1] = edge_in[e].astype(F32)

        finish(run, jnp.int32(2 * run - 1), starts[run] + 2 * run + 1)

    def x_of(o):
        return (wrap(sx + o, side) * side + sy, h)

    def y_of(o):
        return (sx * side + wrap(sy + o, side), h)

    def gather_copies(ref, a, b, halves):
        upper, lower = halves
        one, two = [], []
        for o in range(1, side):
            one.append(remote(
                ref.at[sx, sy, upper], ref.at[sx, sy, upper], a.at[0, o], b.at[0, o], x_of(o)
            ))
            one.append(remote(
                ref.at[sx, sy, lower], ref.at[sx, sy, lower], a.at[1, o], b.at[1, o], y_of(o)
            ))
            two.append(remote(
                ref.at[:, sy, upper], ref.at[:, sy, upper], a.at[2, o], b.at[2, o], y_of(o)
            ))
            two.append(remote(
                ref.at[sx, :, lower], ref.at[sx, :, lower], a.at[3, o], b.at[3, o], x_of(o)
            ))
        return one, two

    def local(ref, sem):
        return pltpu.make_async_copy(ref, ref, sem)

    def gather_arrivals(ref, b, halves):
        upper, lower = halves
        one, two = [], []
        for o in range(1, side):
            fx, fy = wrap(sx - o, side), wrap(sy - o, side)
            one.append(local(ref.at[fx, sy, upper], b.at[0, o]))
            one.append(local(ref.at[sx, fy, lower], b.at[1, o]))
            two.append(local(ref.at[:, fy, upper], b.at[2, o]))
            two.append(local(ref.at[fx, :, lower], b.at[3, o]))
        return one, two

    bias_one, bias_two = gather_copies(far_bias, g_send, g_recv, halves)
    bias_in_one, bias_in_two = gather_arrivals(far_bias, g_recv, halves)

    local(far_bias.at[sx, sy], c_recv.at[0]).wait()
    for copy in bias_one:
        copy.start()

    def bias_steps(i):
        @pl.when(i == 1)
        def _():
            for copy in bias_in_one:
                copy.wait()
            for copy in bias_two:
                copy.start()

    def scatter_one(k):
        copies = []
        for o in range(1, side):
            copies.append(remote(
                parts.at[k, wrap(sx + o, side), :, upper], first_a.at[k, o - 1],
                r_send.at[k, 0, o], r_recv.at[k, 0, o], x_of(o),
            ))
            copies.append(remote(
                parts.at[k, :, wrap(sy + o, side), lower], first_b.at[k, o - 1],
                r_send.at[k, 1, o], r_recv.at[k, 1, o], y_of(o),
            ))
        return copies

    def scatter_two(k):
        copies = []
        for o in range(1, side):
            copies.append(remote(
                mid_a.at[k, wrap(sy + o, side)], second_a.at[k, o - 1],
                r_send.at[k, 2, o], r_recv.at[k, 2, o], y_of(o),
            ))
            copies.append(remote(
                mid_b.at[k, wrap(sx + o, side)], second_b.at[k, o - 1],
                r_send.at[k, 3, o], r_recv.at[k, 3, o], x_of(o),
            ))
        return copies

    def begin_sums(run):
        k = edge_ids[run]

        copies = scatter_one(k)
        for o in (1, 2, 3, 0):
            px = wrap(sx + o, side)

            def part(py, carry, px=px):
                at = latest(run, px * side + py, 2 * H)
                parts[k, px, py] = jnp.where(at >= 0, chain[jnp.maximum(at, 0)], 0.0).astype(BF16)
                return carry

            lax.fori_loop(0, side, part, 0)
            if o:
                copies[2 * o - 2].start()
        for copy in copies[1::2]:
            copy.start()

    def middle_sums(run):
        k = edge_ids[run]
        for o in range(1, side):
            local(first_a.at[k, o - 1], r_recv.at[k, 0, o]).wait()
            local(first_b.at[k, o - 1], r_recv.at[k, 1, o]).wait()
        for i in range(side):
            a = parts[k, sx, i, upper].astype(F32)
            b = parts[k, i, sy, lower].astype(F32)
            for o in range(side - 1):
                a = a + first_a[k, o, i].astype(F32)
                b = b + first_b[k, o, i].astype(F32)
            mid_a[k, i] = a.astype(BF16)
            mid_b[k, i] = b.astype(BF16)
        for copy in scatter_two(k):
            copy.start()

    def end_sums(run):
        k = edge_ids[run]
        for o in range(1, side):
            local(second_a.at[k, o - 1], r_recv.at[k, 2, o]).wait()
            local(second_b.at[k, o - 1], r_recv.at[k, 3, o]).wait()
        a = mid_a[k, sy].astype(F32)
        b = mid_b[k, sx].astype(F32)
        for o in range(side - 1):
            a = a + second_a[k, o].astype(F32)
            b = b + second_b[k, o].astype(F32)
        return a, b

    own_copy(0).wait()
    arrival(starts[near] + 1 + near - c).wait()
    work(near, lambda t: near_bias[t], 0, near, bias_steps)

    own_copy(planes // 2).wait()
    arrival(starts[far] + 1 + far - c).wait()
    for copy in bias_in_two:
        copy.wait()
    work(far, lambda t: far_bias[t // side, lax.rem(t, side)], 0, 2 * far, lambda i: None)
    begin_sums(far)
    passed_over(far)

    def sum_steps(i):
        @pl.when(i == near + 2)
        def _():
            middle_sums(far)

    work(near, lambda t: near_bias[t], near, 2 * near, sum_steps)
    begin_sums(near)
    far_a, far_b = end_sums(far)
    crossed[0, upper] = far_a.astype(BF16)
    crossed[0, lower] = far_b.astype(BF16)
    cross_sum = remote(
        crossed.at[0], crossed.at[1], c_send.at[1], c_recv.at[1], (s, far_head)
    )
    cross_sum.start()
    passed_over(near)
    last_of(far)
    last_of(near)
    gate = jax.nn.sigmoid(gin[...].astype(F32))
    gated[...] = dmix[...].astype(F32) * gate * (1.0 - gate)
    middle_sums(near)
    own_a, own_b = end_sums(near)
    local(crossed.at[1], c_recv.at[1]).wait()
    sums = jnp.concatenate([own_a, own_b], axis=0) + crossed[1].astype(F32)
    dbias_ref[sx, sy] = sums.T.astype(BF16)
    out_one, out_two = gather_copies(dbias_ref, a_send, a_recv, out_halves)
    in_one, in_two = gather_arrivals(dbias_ref, a_recv, out_halves)
    for copy in out_one:
        copy.start()
    for copy in in_one:
        copy.wait()
    for copy in out_two:
        copy.start()

    for head in range(H):
        back_arrival(head).wait()
    attended = got[:, pl.ds(0, DH), :].astype(F32)
    got[:, pl.ds(0, DH), :] = (gated[...] * attended).astype(BF16)
    chunk = 256

    def product(m, carry):
        rows = pl.ds(pl.multiple_of(m * chunk, chunk), chunk)
        acc = jnp.zeros((chunk, PAIR), F32)
        for i, w in enumerate((wg, wq, wk, wv)):
            grads = got[:, pl.ds(i * DH, DH), :].reshape(D, PAIR)
            acc = acc + mm(w[rows, :], grads, ((1,), (0,)))
        dnorm[rows, :] = acc
        return carry

    lax.fori_loop(0, D // chunk, product, 0)
    for piece in range(2):
        rows = pl.ds(piece * BLOCK, BLOCK)
        g = dnorm[:, rows].T * gain
        xhat = scaled[rows, :]
        centre = jnp.mean(g, axis=1, keepdims=True)
        along = jnp.mean(g * xhat, axis=1, keepdims=True)
        dact_ref[rows, :] = (inverse[rows, :1] * (g - centre - xhat * along)).astype(BF16)

    for copy in in_two:
        copy.wait()

    for d, ch in sends:
        if d in (0, planes // 2):
            @pl.when(c != ch)
            def _(d=d, ch=ch):
                forward_copy(d, ch).wait_send()
        else:
            forward_copy(d, ch).wait_send()
    cross_bias.wait_send()
    cross_sum.wait_send()
    for copy in bias_one + bias_two + out_one + out_two:
        copy.wait_send()
    for k in range(2):
        for copy in scatter_one(k) + scatter_two(k):
            copy.wait_send()

    @pl.when(gives_start)
    def _():
        for run in (near, far):
            for ch in range(2):
                key_start(run, ch).wait_send()

    for run in (near, far):
        @pl.when(crosses(run) & (s < S - 1))
        def _(run=run):
            key_wrap(run).wait_send()

        @pl.when(crosses(run) & (s > 0))
        def _(run=run):
            grad_wrap(run).wait_send()

        @pl.when(has_start(run))
        def _(run=run):
            grad_start(run).wait_send()

        for p in range(2 * run):
            if p in (run - 1, run):
                @pl.when(p != run - 1 + c)
                def _(run=run, p=p):
                    back_copy(run, p).wait_send()
            else:
                back_copy(run, p).wait_send()


def shards(H, S, activations, ln_gain, w_query, w_key, w_value, w_gate, w_out, bias_tiles,
           crop_lengths, tile_index, d_out):
    rows, D = activations.shape
    DH = D // H
    tiles = bias_tiles.shape[0]
    crops = crop_lengths.shape[0]
    vmem = pl.BlockSpec(memory_space=pltpu.VMEM)
    smem = pl.BlockSpec(memory_space=pltpu.SMEM)
    hbm = pl.BlockSpec(memory_space=pl.ANY)
    dma = pltpu.SemaphoreType.DMA
    side = math.isqrt(S)
    slots = H + 2
    d_act, d_bias = pl.pallas_call(
        functools.partial(kernel, H, S, DH),
        out_shape=(
            jax.ShapeDtypeStruct((rows, D), BF16),
            jax.ShapeDtypeStruct((side, side, BLOCK, PAIR), BF16),
        ),
        in_specs=[hbm, vmem, hbm, hbm, hbm, hbm, hbm, hbm, hbm, smem, smem],
        out_specs=(vmem, vmem),
        scratch_shapes=[
            pltpu.VMEM((rows, D), BF16),
            pltpu.VMEM((rows, D), BF16),
            pltpu.VMEM((tiles, BLOCK, PAIR), BF16),
            pltpu.VMEM((BLOCK, PAIR), BF16),
            pltpu.VMEM((PAIR, BLOCK), BF16),
            pltpu.VMEM((tiles, PAIR, BLOCK), BF16),
            pltpu.VMEM((side, side, PAIR, BLOCK), BF16),
            pltpu.SMEM((2 * H,), jnp.int32),
            *[pltpu.VMEM((D, D), BF16) for _ in range(5)],
            pltpu.VMEM((rows, D), BF16),
            pltpu.VMEM((rows, D), F32),
            pltpu.VMEM((rows, 128), F32),
            pltpu.VMEM((H, DH, PAIR), BF16),
            pltpu.VMEM((H, DH, PAIR), BF16),
            pltpu.VMEM((H, 4 * DH, PAIR), BF16),
            pltpu.VMEM((slots + 2, 4 * DH, PAIR), BF16),
            pltpu.VMEM((slots, 4 * DH, PAIR), BF16),
            pltpu.VMEM((H, 4 * DH, PAIR), BF16),
            pltpu.VMEM((slots, 2 * DH, PAIR), F32),
            pltpu.VMEM((slots + 3, 2 * DH, BLOCK), F32),
            pltpu.VMEM((2 * H, PAIR, BLOCK), F32),
            pltpu.VMEM((H + 1, crops, PAIR), BF16),
            pltpu.VMEM((H + 1, crops, PAIR), BF16),
            pltpu.VMEM((4, 2 * DH, BLOCK), BF16),
            pltpu.VMEM((4, 2 * DH, BLOCK), BF16),
            pltpu.VMEM((2, side, side, PAIR, BLOCK), BF16),
            pltpu.VMEM((2, side - 1, side, BLOCK, BLOCK), BF16),
            pltpu.VMEM((2, side - 1, side, BLOCK, BLOCK), BF16),
            pltpu.VMEM((2, side, BLOCK, BLOCK), BF16),
            pltpu.VMEM((2, side, BLOCK, BLOCK), BF16),
            pltpu.VMEM((2, side - 1, BLOCK, BLOCK), BF16),
            pltpu.VMEM((2, side - 1, BLOCK, BLOCK), BF16),
            pltpu.VMEM((2, PAIR, BLOCK), BF16),
            pltpu.VMEM((D, PAIR), F32),
            pltpu.VMEM((H, DH, PAIR), F32),
            dma((14,)),
            dma((H,)), dma((slots,)), dma((slots,)), dma((H,)),
            dma((6,)), dma((4,)), dma((4,)), dma((4,)), dma((2,)), dma((2,)),
            dma((4, side)), dma((4, side)), dma((2, 4, side)), dma((2, 4, side)),
            dma((4, side)), dma((4, side)),
        ],
        compiler_params=pltpu.CompilerParams(
            collective_id=0, has_side_effects=True, vmem_limit_bytes=60 * 2**20
        ),
    )(
        activations, ln_gain, d_out, w_query, w_key, w_value, w_gate, w_out,
        bias_tiles.reshape(tiles, BLOCK, PAIR), crop_lengths, tile_index,
    )
    return d_act, d_bias.astype(F32).reshape(tiles, 1, BLOCK, PAIR)


def solution(mesh):
    return jax.shard_map(
        functools.partial(shards, mesh.shape["head"], mesh.shape["seq"]),
        mesh=mesh,
        in_specs=(
            P(("seq", "head"), None),
            P(),
            P(),
            P(),
            P(),
            P(),
            P(),
            P(None, "head", None, None),
            P(),
            P("seq"),
            P(("seq", "head"), None),
        ),
        out_specs=(P(("seq", "head"), None), P(None, "head", None, None)),
        check_vma=False,
    )
```

```python
import functools
import math

import jax
import jax.numpy as jnp
from jax import lax
from jax.experimental import pallas as pl
from jax.experimental.pallas import tpu as pltpu
from jax.sharding import PartitionSpec as P

MESH = pl.DeviceIdType.MESH
F32 = jnp.float32
BF16 = jnp.bfloat16
EPS = 1e-05
UNSEEN = -1e30
BLOCK = 128
PAIR = 2 * BLOCK


def mm(a, b, dims):
    return lax.dot_general(a, b, (dims, ((), ())), preferred_element_type=F32)


def kernel(
    H, S, DH,
    act_hbm, gain_ref, dout_hbm, wq_hbm, wk_hbm, wv_hbm, wg_hbm, wo_hbm, bias_hbm,
    lengths_ref, tiles_ref,
    dact_ref, dbias_ref,
    act, dout, bias, tile, own_tile, near_bias, far_bias, order, wq, wk, wv, wg, wo, normed, scaled, inverse, gin, dmix,
    send, recv, res, got, own, nxt, chain, hotq, hotk, edge_out, edge_in,
    parts, first_a, first_b, mid_a, mid_b, second_a, second_b, crossed, dnorm, gated,
    w_sem, f_send, f_recv, b_send, b_recv, k_send, k_recv, e_send, e_recv, c_send, c_recv,
    g_send, g_recv, r_send, r_recv, a_send, a_recv,
):
    s, h = lax.axis_index("seq"), lax.axis_index("head")
    side = math.isqrt(S)
    planes = H // 2
    sx, sy = s // side, lax.rem(s, side)
    z, c = h // 2, lax.rem(h, 2)
    D = H * DH
    half_heads = H // 2
    half_cols = half_heads * DH
    scale = 1.0 / math.sqrt(DH)
    q_rows, k_rows, v_rows, g_rows = (pl.ds(i * DH, DH) for i in range(4))
    kv_rows = pl.ds(DH, 2 * DH)
    last_block = pl.ds(BLOCK, BLOCK)
    out_halves = pl.ds(0, BLOCK // 2), pl.ds(BLOCK // 2, BLOCK // 2)
    halves = pl.ds(0, BLOCK), pl.ds(BLOCK, BLOCK)
    upper, lower = halves
    near, far = 5, 3
    starts = {near: 0, far: 2 * near + 1}
    total_slots = 2 * near + 2 * far + 2
    wraps = {near: total_slots, far: total_slots + 1}
    nxt_wraps = {near: total_slots + 1, far: total_slots + 2}

    def wrap(i, n):
        return lax.rem(i + n, n)

    other = wrap(z + planes // 2, planes)
    far_head = 2 * other + c
    heads_of = {near: h, far: far_head}

    def remote(src, dst, a, b, device):
        return pltpu.make_async_remote_copy(
            src, dst, a, b, device_id=device, device_id_type=MESH
        )

    mine = pl.ds(pl.multiple_of(h // half_heads * half_cols, 128), half_cols)
    rest = pl.ds(pl.multiple_of((1 - h // half_heads) * half_cols, 128), half_cols)
    loads = [pltpu.make_async_copy(act_hbm, act, w_sem.at[0])]
    for turn, cols in enumerate((mine, rest)):
        for i, (a, b) in enumerate(((wq_hbm, wq), (wk_hbm, wk), (wv_hbm, wv), (wg_hbm, wg))):
            loads.append(
                pltpu.make_async_copy(a.at[:, cols], b.at[:, cols], w_sem.at[1 + 5 * turn + i])
            )
        loads.append(
            pltpu.make_async_copy(wo_hbm.at[cols, :], wo.at[cols, :], w_sem.at[5 + 5 * turn])
        )
    dout_load = pltpu.make_async_copy(dout_hbm, dout, w_sem.at[11])
    bias_load = pltpu.make_async_copy(bias_hbm, bias, w_sem.at[12])
    tile_load = pltpu.make_async_copy(bias_hbm.at[s], tile, w_sem.at[13])
    for load in loads[:6]:
        load.start()
    tile_load.start()
    dout_load.start()
    for load in loads[6:]:
        load.start()
    bias_load.start()

    barrier = pltpu.get_barrier_semaphore()

    def greet(device):
        pl.semaphore_signal(barrier, inc=1, device_id=device, device_id_type=MESH)

    for o in range(1, H):
        greet((s, wrap(h + o, H)))
    for o in range(1, side):
        greet((wrap(sx + o, side) * side + sy, h))
        greet((sx * side + wrap(sy + o, side), h))
    greet((wrap(s + 1, S), h))
    greet((wrap(s + S - 1, S), h))
    at_end = (z == planes - 1) & (c == 1)
    begins = (z == 1) | (z == 2)

    @pl.when(at_end)
    def _():
        for zo in (1, 2):
            for ch in range(2):
                greet((wrap(s + 1, S), 2 * zo + ch))

    @pl.when(begins)
    def _():
        greet((wrap(s + S - 1, S), H - 1))
        greet((wrap(s + S - 1, S), far_head))

    ends = (z == 1 + planes // 2) | (z == 2 + planes // 2)

    @pl.when(ends)
    def _():
        greet((wrap(s + 1, S), far_head))

    greeted = (
        H - 1 + 2 * (side - 1) + 2
        + jnp.where(at_end, 4, 0) + jnp.where(begins, 2, 0) + jnp.where(ends, 1, 0)
    )

    gain = gain_ref[...].astype(F32).reshape(1, D)
    loads[0].wait()
    x = act[...].astype(F32)
    centred = x - jnp.mean(x, axis=1, keepdims=True)
    inv = lax.rsqrt(jnp.mean(centred * centred, axis=1, keepdims=True) + EPS)
    xhat = centred * inv
    scaled[...] = xhat
    inverse[...] = jnp.broadcast_to(inv, inverse.shape)
    normed[...] = (xhat * gain).astype(BF16)

    def target(d):
        if d in (0, 1, 2, planes - 2, planes - 1):
            return d, starts[near] + 1 + 2 * ((near // 2 - d) % planes)
        return (d + planes // 2) % planes, starts[far] + 1 + 2 * ((far // 2 - d - planes // 2) % planes)

    def forward_copy(d, ch):
        up, place = target(d)
        head = 2 * wrap(z + d, planes) + ch
        return remote(
            send.at[head], recv.at[place + c], f_send.at[2 * d + ch], f_recv.at[place + c],
            (s, 2 * wrap(z + up, planes) + ch),
        )

    def own_copy(d):
        place = target(d)[1] + c
        head = 2 * wrap(z + d, planes) + c
        return pltpu.make_async_copy(send.at[head], recv.at[place], f_recv.at[place])

    def arrival(place):
        return pltpu.make_async_copy(recv.at[place], recv.at[place], f_recv.at[place])

    close = [(d, ch) for d in (0, 1, planes - 1, 4, 5, 3) for ch in range(2)]
    distant = [(d, ch) for d in (2, planes - 2) for ch in range(2)]
    sends = close + distant

    def send_some(which, half):
        for d, ch in which:
            head = 2 * wrap(z + d, planes) + ch
            now = True if half is None else head // half_heads == half
            if d in (0, planes // 2):
                now = now & (c != ch)
            if now is True:
                forward_copy(d, ch).start()
            else:
                @pl.when(now)
                def _(d=d, ch=ch):
                    forward_copy(d, ch).start()

    def by_head(product):
        return product.astype(BF16).T.reshape(half_heads, DH, PAIR)

    cross_bias = remote(
        own_tile, far_bias.at[sx, sy], c_send.at[0], c_recv.at[0], (s, far_head)
    )
    tile_load.wait()
    own_tile[...] = tile[...].astype(F32).T.astype(BF16)
    pl.semaphore_wait(barrier, greeted)
    cross_bias.start()
    my_half = h // half_heads
    for turn in range(2):
        half = my_half if turn == 0 else 1 - my_half
        cols = mine if turn == 0 else rest
        heads = pl.ds(half * half_heads, half_heads)
        rows_in = normed[...]
        for i, (w, rows) in enumerate(((wq, q_rows), (wk, k_rows), (wv, v_rows))):
            loads[1 + 5 * turn + i].wait()
            send[heads, rows, :] = by_head(mm(rows_in, w[:, cols], ((1,), (0,))))
        for load in loads[4 + 5 * turn:6 + 5 * turn]:
            load.wait()
        if turn == 0:
            dout_load.wait()
        gate_in = by_head(mm(rows_in, wg[:, cols], ((1,), (0,))))
        mixed = mm(wo[cols, :], dout[...], ((1,), (1,))).astype(BF16)
        mixed = mixed.reshape(half_heads, DH, PAIR)
        gin[heads] = gate_in
        dmix[heads] = mixed
        gate = jax.nn.sigmoid(gate_in.astype(F32))
        send[heads, g_rows, :] = (mixed.astype(F32) * gate).astype(BF16)
        if turn == 0:
            own_copy(0).start()
        else:
            own_copy(planes // 2).start()
        send_some(close, half)

    def key_start(run, ch):
        up = run // 2 + 1
        zo = wrap(z + up, planes)
        head = 2 * (zo if run == near else wrap(zo + planes // 2, planes)) + ch
        group = wrap(s + jnp.where(z == planes - 1, 1, 0), S)
        i = 0 if run == near else 1
        return remote(
            send.at[head, kv_rows, last_block], recv.at[starts[run], kv_rows, last_block],
            k_send.at[2 * i + ch], k_recv.at[i], (group, 2 * zo + ch),
        )

    gives_start = (c == 1) & ((z < planes - 1) | (s < S - 1))

    @pl.when(gives_start)
    def _():
        for ch in range(2):
            key_start(far, ch).start()

    send_some(distant, None)

    @pl.when(gives_start)
    def _():
        for ch in range(2):
            key_start(near, ch).start()

    crops = lengths_ref.shape[0]
    row = lax.broadcasted_iota(jnp.int32, (crops, PAIR), 0)
    lane = lax.broadcasted_iota(jnp.int32, (crops, PAIR), 1)
    low = jnp.zeros((crops, PAIR), jnp.int32)
    high = jnp.zeros((crops, PAIR), jnp.int32)
    total = jnp.int32(0)
    for crop in range(crops):
        low = jnp.where(row == crop, total, low)
        total = total + lengths_ref[crop]
        high = jnp.where(row == crop, total, high)
    for j in range(H + 1):
        pos = (s * H + j - 1) * PAIR + lane
        inside = (pos >= low) & (pos < high)
        hotq[j] = jnp.where(inside, 1.0, 0.0).astype(BF16)
        hotk[j] = jnp.where(inside, 0.0, UNSEEN).astype(BF16)

    def first_pair(run):
        return 2 * wrap(z - run // 2, planes)

    order_at = {near: 0, far: 4 * near}
    for run in (near, far):
        for i in range(2 * run):
            p = run + i // 2 if i % 2 == 0 else run - 1 - i // 2
            j = wrap(first_pair(run) + p, H)
            for b in range(2):
                order[order_at[run] + 2 * i + b] = tiles_ref[2 * j + b]

    def latest(run, tile, before):
        found = jnp.int32(-1)
        for slot in range(order_at[run], order_at[run] + 4 * run):
            found = jnp.where((order[slot] == tile) & (slot < before), slot, found)
        return found

    chain[0] = jnp.zeros((PAIR, BLOCK), F32)

    def turn_tile(n, carry):
        near_bias[n] = bias[n].T
        return carry

    bias_load.wait()
    lax.fori_loop(0, bias.shape[0], turn_tile, 0)

    edge_ids = {near: 0, far: 1}

    def has_start(run):
        return (s > 0) | (first_pair(run) != 0)

    def ends_group(run):
        return wrap(first_pair(run) + 2 * run - 1, H) == H - 1

    def has_end(run):
        return (s < S - 1) | jnp.logical_not(ends_group(run))

    def crosses(run):
        return (first_pair(run) != 0) & (first_pair(run) + 2 * run > H)

    for run in (near, far):
        @pl.when(jnp.logical_not(has_start(run)))
        def _(run=run):
            recv[starts[run]] = jnp.zeros((4 * DH, PAIR), BF16)

        @pl.when(crosses(run) & (s == 0))
        def _(run=run):
            recv[wraps[run]] = jnp.zeros((4 * DH, PAIR), BF16)

        @pl.when(jnp.logical_not(has_end(run)))
        def _(run=run):
            nxt[starts[run] + 2 * run + 1] = jnp.zeros((2 * DH, BLOCK), F32)

        @pl.when(crosses(run) & (s == S - 1))
        def _(run=run):
            nxt[nxt_wraps[run]] = jnp.zeros((2 * DH, BLOCK), F32)

    def key_wrap(run):
        at = starts[run] + 1 + wrap(H - 1 - first_pair(run), H)
        i = edge_ids[run]
        return remote(
            recv.at[at, kv_rows, last_block], recv.at[wraps[run], kv_rows, last_block],
            k_send.at[4 + i], k_recv.at[2 + i], (wrap(s + 1, S), h),
        )

    def grad_wrap(run):
        i = edge_ids[run]
        return remote(
            edge_out.at[2 + i], edge_in.at[2 + i], e_send.at[2 + i], e_recv.at[2 + i],
            (wrap(s + S - 1, S), h),
        )

    def grad_start(run):
        i = edge_ids[run]
        group = wrap(s - jnp.where(first_pair(run) == 0, 1, 0), S)
        return remote(
            edge_out.at[i], edge_in.at[1 - i], e_send.at[i], e_recv.at[1 - i], (group, far_head)
        )

    def edge_arrival(i):
        return pltpu.make_async_copy(edge_in.at[i], edge_in.at[i], e_recv.at[i])

    def key_arrival(place, i):
        part = recv.at[place, kv_rows, last_block]
        return pltpu.make_async_copy(part, part, k_recv.at[i])

    def back_copy(run, p):
        place = starts[run] + 1 + p
        return remote(
            res.at[place], got.at[heads_of[run]], b_send.at[place], b_recv.at[heads_of[run]],
            (s, wrap(first_pair(run) + p, H)),
        )

    def own_back(run):
        place = starts[run] + 1 + run - 1 + c
        return pltpu.make_async_copy(res.at[place], got.at[heads_of[run]], b_recv.at[heads_of[run]])

    def back_arrival(head):
        return pltpu.make_async_copy(got.at[head], got.at[head], b_recv.at[head])

    def finish(run, p, after):
        place = starts[run] + 1 + p
        later = nxt[after]
        sums = own[place]
        res[place, pl.ds(2 * DH, 2 * DH), pl.ds(0, BLOCK)] = sums[:, :BLOCK].astype(BF16)
        res[place, pl.ds(2 * DH, 2 * DH), last_block] = (sums[:, BLOCK:] + later).astype(BF16)
        mine_too = p == run - 1 + c

        @pl.when(mine_too)
        def _():
            own_back(run).start()

        @pl.when(jnp.logical_not(mine_too))
        def _():
            back_copy(run, p).start()

    def attend(tiles, place, before_place, j, b, slot, before):
        lanes = pl.ds(b * BLOCK, BLOCK)
        q = recv[place, q_rows, lanes]
        g = recv[place, g_rows, lanes]
        if b == 0:
            k = jnp.concatenate(
                [recv[before_place, k_rows, last_block], recv[place, k_rows, lanes]], axis=1
            )
            v = jnp.concatenate(
                [recv[before_place, v_rows, last_block], recv[place, v_rows, lanes]], axis=1
            )
            hot = jnp.concatenate([hotk[j, :, last_block], hotk[j + 1, :, lanes]], axis=1)
        else:
            k = recv[place, k_rows, :]
            v = recv[place, v_rows, :]
            hot = hotk[j + 1]
        q_all = jnp.concatenate([q, hotq[j + 1, :, lanes]], axis=0)
        k_all = jnp.concatenate([k, hot], axis=0)
        scores = mm(k_all, q_all, ((0,), (0,))) * scale + tiles(order[slot]).astype(F32)
        weights = jnp.exp(scores - jnp.max(scores, axis=0, keepdims=True))
        probs = weights * (1.0 / jnp.sum(weights, axis=0, keepdims=True))
        probs_low = probs.astype(BF16)
        d_probs = mm(v, g, ((0,), (0,)))
        d_scores = probs * (d_probs - jnp.sum(probs * d_probs, axis=0, keepdims=True))
        d_low = d_scores.astype(BF16)
        res[place, pl.ds(0, DH), lanes] = mm(v, probs_low, ((1,), (0,))).astype(BF16)
        res[place, pl.ds(DH, DH), lanes] = (mm(k, d_low, ((1,), (0,))) * scale).astype(BF16)
        kept = jnp.where(before >= 0, chain[jnp.maximum(before, 0)], 0.0)
        chain[slot] = kept + d_scores
        d_k = mm(q, d_low, ((1,), (1,))) * scale
        d_v = mm(g, probs_low, ((1,), (1,)))
        return d_k, d_v

    def work(run, tiles, begin, end, beside):
        base = starts[run] + 1
        e = edge_ids[run]
        wraps_at = wrap(H - first_pair(run), H)

        def step(i, carry):
            up = lax.rem(i, 2) == 0
            p = jnp.where(up, run + i // 2, run - 1 - i // 2)
            j = wrap(first_pair(run) + p, H)
            arrived = jnp.where(up, p, p - 1)
            beside(i)

            @pl.when(arrived >= 0)
            def _():
                @pl.when(i > 0)
                def _():
                    arrival(base + arrived).wait()

                @pl.when(crosses(run) & (s < S - 1) & (arrived == wraps_at - 1))
                def _():
                    key_wrap(run).start()

            @pl.when((arrived < 0) & has_start(run))
            def _():
                key_arrival(starts[run], e).wait()

            inner = crosses(run) & (p == wraps_at)

            @pl.when(inner & (s > 0))
            def _():
                key_arrival(wraps[run], 2 + e).wait()

            place = base + p
            before_place = jnp.where(inner, wraps[run], place - 1)
            slot = order_at[run] + 2 * i
            first_k, first_v = attend(
                tiles, place, before_place, j, 0, slot, latest(run, order[slot], slot)
            )
            second_k, second_v = attend(
                tiles, place, before_place, j, 1, slot + 1,
                latest(run, order[slot + 1], slot + 1),
            )
            nxt[place, pl.ds(0, DH), :] = first_k[:, :BLOCK]
            nxt[place, pl.ds(DH, DH), :] = first_v[:, :BLOCK]
            own[place, pl.ds(0, DH), pl.ds(0, BLOCK)] = first_k[:, BLOCK:] + second_k[:, :BLOCK]
            own[place, pl.ds(DH, DH), pl.ds(0, BLOCK)] = first_v[:, BLOCK:] + second_v[:, :BLOCK]
            own[place, pl.ds(0, DH), last_block] = second_k[:, BLOCK:]
            own[place, pl.ds(DH, DH), last_block] = second_v[:, BLOCK:]

            @pl.when(inner & (s > 0))
            def _():
                edge_out[2 + e] = nxt[place].astype(BF16)
                grad_wrap(run).start()

            @pl.when((p == 0) & has_start(run))
            def _():
                edge_out[e] = nxt[place].astype(BF16)
                grad_start(run).start()

            f = jnp.where(up, p - 1, p)

            @pl.when((i > 0) & jnp.logical_not(crosses(run) & (f == wraps_at - 1)))
            def _():
                finish(run, f, starts[run] + 2 + f)

            return carry

        lax.fori_loop(begin, end, step, 0)

    def passed_over(run):
        e = edge_ids[run]

        @pl.when(crosses(run))
        def _():
            @pl.when(s < S - 1)
            def _():
                edge_arrival(2 + e).wait()
                nxt[nxt_wraps[run]] = edge_in[2 + e].astype(F32)

            finish(run, wrap(H - first_pair(run), H) - 1, nxt_wraps[run])

    def last_of(run):
        e = edge_ids[run]

        @pl.when(has_end(run))
        def _():
            edge_arrival(e).wait()
            nxt[starts[run] + 2 * run + 1] = edge_in[e].astype(F32)

        finish(run, jnp.int32(2 * run - 1), starts[run] + 2 * run + 1)

    def x_of(o):
        return (wrap(sx + o, side) * side + sy, h)

    def y_of(o):
        return (sx * side + wrap(sy + o, side), h)

    def gather_copies(ref, a, b, halves):
        upper, lower = halves
        one, two = [], []
        for o in range(1, side):
            one.append(remote(
                ref.at[sx, sy, upper], ref.at[sx, sy, upper], a.at[0, o], b.at[0, o], x_of(o)
            ))
            one.append(remote(
                ref.at[sx, sy, lower], ref.at[sx, sy, lower], a.at[1, o], b.at[1, o], y_of(o)
            ))
            two.append(remote(
                ref.at[:, sy, upper], ref.at[:, sy, upper], a.at[2, o], b.at[2, o], y_of(o)
            ))
            two.append(remote(
                ref.at[sx, :, lower], ref.at[sx, :, lower], a.at[3, o], b.at[3, o], x_of(o)
            ))
        return one, two

    def local(ref, sem):
        return pltpu.make_async_copy(ref, ref, sem)

    def gather_arrivals(ref, b, halves):
        upper, lower = halves
        one, two = [], []
        for o in range(1, side):
            fx, fy = wrap(sx - o, side), wrap(sy - o, side)
            one.append(local(ref.at[fx, sy, upper], b.at[0, o]))
            one.append(local(ref.at[sx, fy, lower], b.at[1, o]))
            two.append(local(ref.at[:, fy, upper], b.at[2, o]))
            two.append(local(ref.at[fx, :, lower], b.at[3, o]))
        return one, two

    bias_one, bias_two = gather_copies(far_bias, g_send, g_recv, halves)
    bias_in_one, bias_in_two = gather_arrivals(far_bias, g_recv, halves)

    local(far_bias.at[sx, sy], c_recv.at[0]).wait()
    for copy in bias_one:
        copy.start()

    def bias_steps(i):
        @pl.when(i == 1)
        def _():
            for copy in bias_in_one:
                copy.wait()
            for copy in bias_two:
                copy.start()

    def scatter_one(k):
        copies = []
        for o in range(1, side):
            copies.append(remote(
                parts.at[k, wrap(sx + o, side), :, upper], first_a.at[k, o - 1],
                r_send.at[k, 0, o], r_recv.at[k, 0, o], x_of(o),
            ))
            copies.append(remote(
                parts.at[k, :, wrap(sy + o, side), lower], first_b.at[k, o - 1],
                r_send.at[k, 1, o], r_recv.at[k, 1, o], y_of(o),
            ))
        return copies

    def scatter_two(k):
        copies = []
        for o in range(1, side):
            copies.append(remote(
                mid_a.at[k, wrap(sy + o, side)], second_a.at[k, o - 1],
                r_send.at[k, 2, o], r_recv.at[k, 2, o], y_of(o),
            ))
            copies.append(remote(
                mid_b.at[k, wrap(sx + o, side)], second_b.at[k, o - 1],
                r_send.at[k, 3, o], r_recv.at[k, 3, o], x_of(o),
            ))
        return copies

    def begin_sums(run):
        k = edge_ids[run]

        copies = scatter_one(k)
        for o in (1, 2, 3, 0):
            px = wrap(sx + o, side)

            def part(py, carry, px=px):
                at = latest(run, px * side + py, 2 * H)
                parts[k, px, py] = jnp.where(at >= 0, chain[jnp.maximum(at, 0)], 0.0).astype(BF16)
                return carry

            lax.fori_loop(0, side, part, 0)
            if o:
                copies[2 * o - 2].start()
        for copy in copies[1::2]:
            copy.start()

    def middle_sums(run):
        k = edge_ids[run]
        for o in range(1, side):
            local(first_a.at[k, o - 1], r_recv.at[k, 0, o]).wait()
            local(first_b.at[k, o - 1], r_recv.at[k, 1, o]).wait()
        for i in range(side):
            a = parts[k, sx, i, upper].astype(F32)
            b = parts[k, i, sy, lower].astype(F32)
            for o in range(side - 1):
                a = a + first_a[k, o, i].astype(F32)
                b = b + first_b[k, o, i].astype(F32)
            mid_a[k, i] = a.astype(BF16)
            mid_b[k, i] = b.astype(BF16)
        for copy in scatter_two(k):
            copy.start()

    def end_sums(run):
        k = edge_ids[run]
        for o in range(1, side):
            local(second_a.at[k, o - 1], r_recv.at[k, 2, o]).wait()
            local(second_b.at[k, o - 1], r_recv.at[k, 3, o]).wait()
        a = mid_a[k, sy].astype(F32)
        b = mid_b[k, sx].astype(F32)
        for o in range(side - 1):
            a = a + second_a[k, o].astype(F32)
            b = b + second_b[k, o].astype(F32)
        return a, b

    own_copy(0).wait()
    arrival(starts[near] + 1 + near - c).wait()
    work(near, lambda t: near_bias[t], 0, near, bias_steps)

    own_copy(planes // 2).wait()
    arrival(starts[far] + 1 + far - c).wait()
    for copy in bias_in_two:
        copy.wait()
    work(far, lambda t: far_bias[t // side, lax.rem(t, side)], 0, 2 * far, lambda i: None)
    begin_sums(far)
    passed_over(far)

    def sum_steps(i):
        @pl.when(i == near + 2)
        def _():
            middle_sums(far)

    work(near, lambda t: near_bias[t], near, 2 * near, sum_steps)
    begin_sums(near)
    far_a, far_b = end_sums(far)
    crossed[0, upper] = far_a.astype(BF16)
    crossed[0, lower] = far_b.astype(BF16)
    cross_sum = remote(
        crossed.at[0], crossed.at[1], c_send.at[1], c_recv.at[1], (s, far_head)
    )
    cross_sum.start()
    passed_over(near)
    last_of(far)
    last_of(near)
    gate = jax.nn.sigmoid(gin[...].astype(F32))
    gated[...] = dmix[...].astype(F32) * gate * (1.0 - gate)
    middle_sums(near)
    own_a, own_b = end_sums(near)
    local(crossed.at[1], c_recv.at[1]).wait()
    sums = jnp.concatenate([own_a, own_b], axis=0) + crossed[1].astype(F32)
    dbias_ref[sx, sy] = sums.T.astype(BF16)
    out_one, out_two = gather_copies(dbias_ref, a_send, a_recv, out_halves)
    in_one, in_two = gather_arrivals(dbias_ref, a_recv, out_halves)
    for copy in out_one:
        copy.start()
    for copy in in_one:
        copy.wait()
    for copy in out_two:
        copy.start()

    for head in range(H):
        back_arrival(head).wait()
    attended = got[:, pl.ds(0, DH), :].astype(F32)
    got[:, pl.ds(0, DH), :] = (gated[...] * attended).astype(BF16)
    chunk = 256

    def product(m, carry):
        rows = pl.ds(pl.multiple_of(m * chunk, chunk), chunk)
        acc = jnp.zeros((chunk, PAIR), F32)
        for i, w in enumerate((wg, wq, wk, wv)):
            grads = got[:, pl.ds(i * DH, DH), :].reshape(D, PAIR)
            acc = acc + mm(w[rows, :], grads, ((1,), (0,)))
        dnorm[rows, :] = acc
        return carry

    lax.fori_loop(0, D // chunk, product, 0)
    for piece in range(2):
        rows = pl.ds(piece * BLOCK, BLOCK)
        g = dnorm[:, rows].T * gain
        xhat = scaled[rows, :]
        centre = jnp.mean(g, axis=1, keepdims=True)
        along = jnp.mean(g * xhat, axis=1, keepdims=True)
        dact_ref[rows, :] = (inverse[rows, :1] * (g - centre - xhat * along)).astype(BF16)

    for copy in in_two:
        copy.wait()

    for d, ch in sends:
        if d in (0, planes // 2):
            @pl.when(c != ch)
            def _(d=d, ch=ch):
                forward_copy(d, ch).wait_send()
        else:
            forward_copy(d, ch).wait_send()
    cross_bias.wait_send()
    cross_sum.wait_send()
    for copy in bias_one + bias_two + out_one + out_two:
        copy.wait_send()
    for k in range(2):
        for copy in scatter_one(k) + scatter_two(k):
            copy.wait_send()

    @pl.when(gives_start)
    def _():
        for run in (near, far):
            for ch in range(2):
                key_start(run, ch).wait_send()

    for run in (near, far):
        @pl.when(crosses(run) & (s < S - 1))
        def _(run=run):
            key_wrap(run).wait_send()

        @pl.when(crosses(run) & (s > 0))
        def _(run=run):
            grad_wrap(run).wait_send()

        @pl.when(has_start(run))
        def _(run=run):
            grad_start(run).wait_send()

        for p in range(2 * run):
            if p in (run - 1, run):
                @pl.when(p != run - 1 + c)
                def _(run=run, p=p):
                    back_copy(run, p).wait_send()
            else:
                back_copy(run, p).wait_send()


def shards(H, S, activations, ln_gain, w_query, w_key, w_value, w_gate, w_out, bias_tiles,
           crop_lengths, tile_index, d_out):
    rows, D = activations.shape
    DH = D // H
    tiles = bias_tiles.shape[0]
    crops = crop_lengths.shape[0]
    vmem = pl.BlockSpec(memory_space=pltpu.VMEM)
    smem = pl.BlockSpec(memory_space=pltpu.SMEM)
    hbm = pl.BlockSpec(memory_space=pl.ANY)
    dma = pltpu.SemaphoreType.DMA
    side = math.isqrt(S)
    slots = H + 2
    d_act, d_bias = pl.pallas_call(
        functools.partial(kernel, H, S, DH),
        out_shape=(
            jax.ShapeDtypeStruct((rows, D), BF16),
            jax.ShapeDtypeStruct((side, side, BLOCK, PAIR), BF16),
        ),
        in_specs=[hbm, vmem, hbm, hbm, hbm, hbm, hbm, hbm, hbm, smem, smem],
        out_specs=(vmem, vmem),
        scratch_shapes=[
            pltpu.VMEM((rows, D), BF16),
            pltpu.VMEM((rows, D), BF16),
            pltpu.VMEM((tiles, BLOCK, PAIR), BF16),
            pltpu.VMEM((BLOCK, PAIR), BF16),
            pltpu.VMEM((PAIR, BLOCK), BF16),
            pltpu.VMEM((tiles, PAIR, BLOCK), BF16),
            pltpu.VMEM((side, side, PAIR, BLOCK), BF16),
            pltpu.SMEM((2 * H,), jnp.int32),
            *[pltpu.VMEM((D, D), BF16) for _ in range(5)],
            pltpu.VMEM((rows, D), BF16),
            pltpu.VMEM((rows, D), F32),
            pltpu.VMEM((rows, 128), F32),
            pltpu.VMEM((H, DH, PAIR), BF16),
            pltpu.VMEM((H, DH, PAIR), BF16),
            pltpu.VMEM((H, 4 * DH, PAIR), BF16),
            pltpu.VMEM((slots + 2, 4 * DH, PAIR), BF16),
            pltpu.VMEM((slots, 4 * DH, PAIR), BF16),
            pltpu.VMEM((H, 4 * DH, PAIR), BF16),
            pltpu.VMEM((slots, 2 * DH, PAIR), F32),
            pltpu.VMEM((slots + 3, 2 * DH, BLOCK), F32),
            pltpu.VMEM((2 * H, PAIR, BLOCK), F32),
            pltpu.VMEM((H + 1, crops, PAIR), BF16),
            pltpu.VMEM((H + 1, crops, PAIR), BF16),
            pltpu.VMEM((4, 2 * DH, BLOCK), BF16),
            pltpu.VMEM((4, 2 * DH, BLOCK), BF16),
            pltpu.VMEM((2, side, side, PAIR, BLOCK), BF16),
            pltpu.VMEM((2, side - 1, side, BLOCK, BLOCK), BF16),
            pltpu.VMEM((2, side - 1, side, BLOCK, BLOCK), BF16),
            pltpu.VMEM((2, side, BLOCK, BLOCK), BF16),
            pltpu.VMEM((2, side, BLOCK, BLOCK), BF16),
            pltpu.VMEM((2, side - 1, BLOCK, BLOCK), BF16),
            pltpu.VMEM((2, side - 1, BLOCK, BLOCK), BF16),
            pltpu.VMEM((2, PAIR, BLOCK), BF16),
            pltpu.VMEM((D, PAIR), F32),
            pltpu.VMEM((H, DH, PAIR), F32),
            dma((14,)),
            dma((H,)), dma((slots,)), dma((slots,)), dma((H,)),
            dma((6,)), dma((4,)), dma((4,)), dma((4,)), dma((2,)), dma((2,)),
            dma((4, side)), dma((4, side)), dma((2, 4, side)), dma((2, 4, side)),
            dma((4, side)), dma((4, side)),
        ],
        compiler_params=pltpu.CompilerParams(
            collective_id=0, has_side_effects=True, vmem_limit_bytes=60 * 2**20
        ),
    )(
        activations, ln_gain, d_out, w_query, w_key, w_value, w_gate, w_out,
        bias_tiles.reshape(tiles, BLOCK, PAIR), crop_lengths, tile_index,
    )
    return d_act, d_bias.astype(F32).reshape(tiles, 1, BLOCK, PAIR)


def solution(mesh):
    return jax.shard_map(
        functools.partial(shards, mesh.shape["head"], mesh.shape["seq"]),
        mesh=mesh,
        in_specs=(
            P(("seq", "head"), None),
            P(),
            P(),
            P(),
            P(),
            P(),
            P(),
            P(None, "head", None, None),
            P(),
            P("seq"),
            P(("seq", "head"), None),
        ),
        out_specs=(P(("seq", "head"), None), P(None, "head", None, None)),
        check_vma=False,
    )
```
